128 devices in a mesh: dp: 16 (over z_hi, x, core), tensor: 8 (over z_lo, y).
Axes of the slice: x: 4, y: 4, z: 4 (z_hi: 2, z_lo: 2; z = z_hi * 2 + z_lo), core: 2. Of those that a mesh axis runs over, the one named last changes fastest.
Arguments:
- residual: bfloat16 [16, 1024, 1024], P('dp', 'tensor')
- segments: int32 [16, 1024], P('dp'), may hold values from 0 to 3, never falling along the last dimension, each value on 1 to 512 neighbouring positions
- first_gain: float32 [2, 1024], replicated, may hold values from 0.25 to 1.75
- first_bias: float32 [2, 1024], replicated, may hold values from -3 to 3
- second_gain: float32 [2, 1024], replicated, may hold values from 0.25 to 1.75
- second_bias: float32 [2, 1024], replicated, may hold values from -3 to 3
- attention_weight: bfloat16 [2, 1024, 3072], P(None, 'dp', 'tensor')
- attention_bias: float32 [2, 2048], P(None, 'tensor'), may hold values from -3 to 3
- project_weight: bfloat16 [2, 1024, 1024], P(None, 'tensor', 'dp'), may hold values from -0.5 to 0.5
- project_bias: float32 [2, 1024], replicated, may hold values from -3 to 3
- expand_weight: bfloat16 [2, 1024, 4096], P(None, 'dp', 'tensor'), may hold values from -0.1875 to 0.1875
- expand_bias: float32 [2, 4096], P(None, 'tensor'), may hold values from -3 to 3
- contract_weight: bfloat16 [2, 4096, 1024], P(None, 'tensor', 'dp'), may hold values from -0.125 to 0.125
- contract_bias: float32 [2, 1024], replicated, may hold values from -3 to 3
- cotangent: float32 [16, 1024, 1024], P('dp', 'tensor'), may hold values from -5 to 5
Outputs:
- result: float32 [16, 1024, 1024], P('dp', 'tensor')
- residual_grad: float32 [16, 1024, 1024], P('dp', 'tensor')
- first_gain_grad: float32 [2, 1024], replicated
- first_bias_grad: float32 [2, 1024], replicated
- second_gain_grad: float32 [2, 1024], replicated
- second_bias_grad: float32 [2, 1024], replicated
- attention_weight_grad: float32 [2, 1024, 3072], P(None, 'dp', 'tensor')
- attention_bias_grad: float32 [2, 2048], P(None, 'tensor')
- project_weight_grad: float32 [2, 1024, 1024], P(None, 'tensor', 'dp')
- project_bias_grad: float32 [2, 1024], replicated
- expand_weight_grad: float32 [2, 1024, 4096], P(None, 'dp', 'tensor')
- expand_bias_grad: float32 [2, 4096], P(None, 'tensor')
- contract_weight_grad: float32 [2, 4096, 1024], P(None, 'tensor', 'dp')
- contract_bias_grad: float32 [2, 1024], replicated
The draws below stay inside these ranges and needn't reach their ends.
Inputs may be any that keep to these rules, and one draw needn't show every extreme that they name: `segments`: in each sequence the segment numbers start at 0 and never fall; a segment holds at most half of 1024 tokens.
All inputs are finite; a program needn't handle non-finite values.
Results may differ from the reference program's by a relative error of at most 0.0095.
Values may be sent and summed in bfloat16 or wider, within the bound.
A program may use at most 192 MiB of HBM per device.

```python
import math
import jax
import jax.numpy as jnp
import numpy as np
from jax import lax

D = 1024
H = 16
FF = 4096
HD = 64
ROT = 16
LEN = 1024
LAYERS = 2
SEQS = 16
N_TENSOR = 8


def draw_residual(key, part):
    keys_split = jax.random.split(key, 3)
    row_scale = jnp.exp(jax.random.uniform(keys_split[0], (SEQS, LEN // 2, 1, 1), jnp.float32, math.log(0.5), math.log(5.0)))
    column_scale = jnp.exp(jax.random.uniform(keys_split[1], (D,), jnp.float32, math.log(0.5), math.log(2.0)))
    entries = jax.random.truncated_normal(keys_split[2], -4.0, 4.0, (SEQS, LEN // 2, 2, D), jnp.float32) * column_scale
    return (entries * row_scale).reshape(SEQS, LEN, D).astype(jnp.bfloat16)


def draw_attention_weight(key, part):
    spread = D ** (-0.5)
    weights = jax.random.truncated_normal(key, -4.0, 4.0, (LAYERS, D, H, 3, HD), jnp.float32) * spread
    return weights.reshape(LAYERS, D, 3 * D).astype(jnp.bfloat16)


def draw_cotangent(key, part):
    keys_split = jax.random.split(key, 3)
    noise = 0.25 * jax.random.truncated_normal(keys_split[0], -6.0, 6.0, (SEQS, LEN, D), jnp.float32)
    block_rows = LEN // N_TENSOR
    owners_count = SEQS * N_TENSOR
    sequence_index = jnp.arange(SEQS).astype(jnp.int32)[:, None]
    token_index = jnp.arange(LEN).astype(jnp.int32)[None, :]
    owner = sequence_index * N_TENSOR + token_index // block_rows
    start_feature = jax.random.randint(keys_split[1], (), 0, D)
    feature = (owner * 37 + start_feature) % D
    sign_bits = jax.random.randint(keys_split[2], (owners_count,), 0, 2)
    signs = (2 * sign_bits - 1).astype(jnp.float32)
    owner_sign = jnp.take(signs, owner)
    columns = jnp.arange(D).astype(jnp.int32)
    heavy = jnp.where(feature[..., None] == columns, 3.0, 0.0) * owner_sign[..., None]
    return (noise + heavy).astype(jnp.float32)


def level_of(rng, extent, pieces, low, largest):
    loudness, own = 1.0, jax.random.fold_in(rng, 6)
    for axis_at, blocks in pieces:
        steps = jnp.exp(jax.random.uniform(jax.random.fold_in(own, axis_at), (blocks,), jnp.float32, low / len(pieces), largest / len(pieces)))
        loudness = loudness * jnp.repeat(steps, extent[axis_at] // blocks).reshape([-1 if axis == axis_at else 1 for axis in range(len(extent))])
    return loudness


def split_up(count, total, most, slope):
    loads = [(1 << 20) // math.isqrt(grade ** slope) + 1 for grade in range(2, count + 1)]
    rest, counts = total - most - (count - 1), [1] * (count - 1)
    while rest > 0:
        movable = [i for i in range(count - 1) if counts[i] < most]
        whole, budget = sum([loads[i] for i in movable]), rest
        for i in movable:
            addition = min(most - counts[i], max(1, budget * loads[i] // whole), rest)
            counts[i] = counts[i] + addition
            rest = rest - addition
    return np.array([most] + counts)


def ragged(key, amount, total, reach, skew):
    if amount == 2:
        one = jax.random.randint(key, (), max(1, total - reach), min(reach, total - 1) + 1)
        return jnp.stack([one, total - one])
    tallies = jnp.asarray(split_up(amount, total, reach, skew), jnp.int32)
    twos = (amount - 1) // 2
    source_of, taker = tallies[1:1 + 2 * twos:2], tallies[2:2 + 2 * twos:2]
    slack = jnp.minimum(source_of - 1, reach - taker)
    passed = jax.random.randint(jax.random.fold_in(key, 1), (twos,), 0, 1 << 20) % (slack + 1)
    tallies = tallies.at[1:1 + 2 * twos:2].set(source_of - passed).at[2:2 + 2 * twos:2].set(taker + passed)
    return tallies[jax.random.permutation(jax.random.fold_in(key, 2), amount)]


def normal_values(key, dims, width, reach, cuts=(), kind=jnp.bfloat16):
    factor_of = level_of(key, dims, cuts, -0.22, 0.18) if cuts else 1.0
    drawn = jax.random.normal(key, dims, jnp.float32) * width * factor_of
    return jnp.minimum(jnp.maximum(drawn, -reach), reach).astype(kind)


def setup_inputs(seed: int = 0) -> dict:
    seeds = jax.random.split(jax.random.key(seed), 16)
    return {
        "residual": draw_residual(jax.random.fold_in(seeds[15], 71), 0),
        "segments": jax.vmap(lambda own: jnp.searchsorted(jnp.cumsum(ragged(own, 4, LEN, LEN // 2, 1)), jnp.arange(LEN), side="right"))(jax.random.split(seeds[1], SEQS)).reshape((SEQS, LEN)).astype(jnp.int32),
        "first_gain": jnp.clip(1.0 + 0.15 * jax.random.normal(seeds[2], (LAYERS, D), jnp.float32), 0.25, 1.75),
        "first_bias": normal_values(seeds[3], (LAYERS, D), 0.5, 3.0, (), jnp.float32),
        "second_gain": jnp.clip(1.0 + 0.15 * jax.random.normal(seeds[4], (LAYERS, D), jnp.float32), 0.25, 1.75),
        "second_bias": normal_values(seeds[5], (LAYERS, D), 0.5, 3.0, (), jnp.float32),
        "attention_weight": draw_attention_weight(jax.random.fold_in(seeds[15], 71), 0),
        "attention_bias": normal_values(seeds[7], (LAYERS, 2 * D), 0.5, 3.0, ((1, 8),), jnp.float32),
        "project_weight": normal_values(seeds[8], (LAYERS, D, D), (D // 8) ** -0.5, 0.5, ((1, 8), (2, 16))),
        "project_bias": normal_values(seeds[9], (LAYERS, D), 0.5, 3.0, (), jnp.float32),
        "expand_weight": normal_values(seeds[10], (LAYERS, D, FF), D ** -0.5, 0.1875, ((1, 16), (2, 8))),
        "expand_bias": normal_values(seeds[11], (LAYERS, FF), 0.5, 3.0, ((1, 8),), jnp.float32),
        "contract_weight": normal_values(seeds[12], (LAYERS, FF, D), (FF // 2) ** -0.5, 0.125, ((1, 8), (2, 16))),
        "contract_bias": normal_values(seeds[13], (LAYERS, D), 0.5, 3.0, (), jnp.float32),
        "cotangent": draw_cotangent(jax.random.fold_in(seeds[15], 71), 0),
    }


epsilon = 1e-05
root_half = 0.7071067811865476
gauss_norm = 0.3989422804014327
masked_score = -1e+30

def rotary_tables(segment_row):
    length = segment_row.shape[0]
    places = jnp.arange(length).astype(jnp.int32)
    starts_here = jnp.concatenate([jnp.ones((1,), dtype=jnp.bool_), segment_row[1:] != segment_row[:-1]])
    first_place = lax.cummax(jnp.where(starts_here, places, jnp.zeros_like(places)), axis=0)
    offset = (places - first_place).astype(jnp.float32)
    halfway = ROT // 2
    frequency = jnp.power(10000.0, -(jnp.arange(halfway).astype(jnp.float32) * 2.0 / ROT))
    angles = offset[:, None] * frequency[None, :]
    angles = jnp.concatenate([angles, angles], axis=1)
    return (jnp.cos(angles), jnp.sin(angles))

def rotate_half(values):
    halfway = values.shape[-1] // 2
    return jnp.concatenate([-values[..., halfway:], values[..., :halfway]], axis=-1)

def rotate(values, cosine_table, sine_table):
    moving = values[..., :ROT]
    return jnp.concatenate([moving * cosine_table + rotate_half(moving) * sine_table, values[..., ROT:]], axis=-1)

def unrotate(grads, cosine_table, sine_table):
    moving = grads[..., :ROT]
    return jnp.concatenate([moving * cosine_table - rotate_half(moving * sine_table), grads[..., ROT:]], axis=-1)

def gelu_value(hidden):
    return 0.5 * hidden * (1.0 + lax.erf(hidden * root_half))

def gelu_slope(hidden):
    return 0.5 * (1.0 + lax.erf(hidden * root_half)) + hidden * jnp.exp(-0.5 * hidden * hidden) * gauss_norm

def allowed_block(segments, first_row, block_rows):
    length = segments.shape[-1]
    key_place = jnp.arange(length).astype(jnp.int32)
    query_place = first_row + jnp.arange(block_rows).astype(jnp.int32)
    query_segment = segments[..., first_row:first_row + block_rows]
    same_segment = query_segment[..., :, None] == segments[..., None, :]
    return same_segment & (key_place[None, :] <= query_place[:, None])

def rounded_wide(values):
    return lax.optimization_barrier(values.astype(jnp.bfloat16)).astype(jnp.float32)

def layer_norm_parts(stream):
    centre = stream - lax.optimization_barrier(jnp.mean(stream, axis=-1, keepdims=True))
    inv_std = lax.rsqrt(lax.optimization_barrier(jnp.mean(centre * centre, axis=-1, keepdims=True)) + epsilon)
    return (centre * inv_std, inv_std)

def attention_forward(queries, keys, values, segments):
    length = segments.shape[-1]
    block_rows = min(512, length)
    keys_wide = keys.astype(jnp.float32)
    values_wide = values.astype(jnp.float32)
    outputs = []
    totals = []
    for first_row in range(0, length, block_rows):
        keep_mask = allowed_block(segments, first_row, block_rows)[:, None]
        query_rows = queries[:, first_row:first_row + block_rows].astype(jnp.float32)
        scores = jnp.einsum('bqhe,bkhe->bhqk', query_rows, keys_wide) * HD ** (-0.5)
        scores = jnp.where(keep_mask, scores, masked_score)
        row_max = lax.optimization_barrier(jnp.max(scores, axis=-1, keepdims=True))
        row_total = row_max + jnp.log(lax.optimization_barrier(jnp.sum(jnp.exp(scores - row_max), axis=-1, keepdims=True)))
        attention_weights = rounded_wide(jnp.where(keep_mask, jnp.exp(scores - row_total), 0.0))
        outputs.append(jnp.einsum('bhqk,bkhe->bqhe', attention_weights, values_wide).astype(jnp.bfloat16))
        totals.append(row_total[..., 0])
    return (jnp.concatenate(outputs, axis=1), jnp.concatenate(totals, axis=2))

def attention_backward(queries, keys, values, mixed, mixed_grad, totals, segments):
    length = segments.shape[-1]
    block_rows = min(512, length)
    keys_wide = keys.astype(jnp.float32)
    values_wide = values.astype(jnp.float32)
    query_parts = []
    key_grad = jnp.zeros(keys.shape, jnp.float32)
    value_grad = jnp.zeros(values.shape, jnp.float32)
    for first_row in range(0, length, block_rows):
        keep_mask = allowed_block(segments, first_row, block_rows)[:, None]
        query_rows = queries[:, first_row:first_row + block_rows].astype(jnp.float32)
        grad_rows = mixed_grad[:, first_row:first_row + block_rows].astype(jnp.float32)
        out_rows = mixed[:, first_row:first_row + block_rows].astype(jnp.float32)
        total_rows = totals[:, :, first_row:first_row + block_rows]
        scores = jnp.einsum('bqhe,bkhe->bhqk', query_rows, keys_wide) * HD ** (-0.5)
        scores = jnp.where(keep_mask, scores, masked_score)
        soft_weights = jnp.where(keep_mask, jnp.exp(scores - total_rows[..., None]), 0.0)
        prob_grad = jnp.einsum('bqhe,bkhe->bhqk', grad_rows, values_wide)
        row_delta = jnp.einsum('bqhe,bqhe->bhq', grad_rows, out_rows)
        score_grad = rounded_wide(soft_weights * (prob_grad - row_delta[..., None]) * HD ** (-0.5))
        query_parts.append(jnp.einsum('bhqk,bkhe->bqhe', score_grad, keys_wide))
        key_grad = key_grad + jnp.einsum('bhqk,bqhe->bkhe', score_grad, query_rows)
        value_grad = value_grad + jnp.einsum('bhqk,bqhe->bkhe', rounded_wide(soft_weights), grad_rows)
    return (jnp.concatenate(query_parts, axis=1), key_grad, value_grad)

def forward_one(sequence_items):
    queries, keys, values, segment_row = sequence_items
    mixed, totals = attention_forward(queries[None], keys[None], values[None], segment_row[None])
    return (mixed[0], totals[0])

def backward_one(sequence_items):
    queries, keys, values, mixed, mixed_grad, totals, segment_row = sequence_items
    query_grad, key_grad, value_grad = attention_backward(queries[None], keys[None], values[None], mixed[None], mixed_grad[None], totals[None], segment_row[None])
    return (query_grad[0], key_grad[0], value_grad[0])

def reference(residual, segments, first_gain, first_bias, second_gain, second_bias, attention_weight, attention_bias, project_weight, project_bias, expand_weight, expand_bias, contract_weight, contract_bias, cotangent):
    cosine_table, sine_table = jax.vmap(rotary_tables)(segments)
    cosine_table = cosine_table[:, :, None, :]
    sine_table = sine_table[:, :, None, :]
    stream = residual.astype(jnp.float32)
    saved = []
    for layer_at in range(LAYERS):
        normed_hat, inv_std = layer_norm_parts(stream)
        first_normed = (normed_hat * first_gain[layer_at] + first_bias[layer_at]).astype(jnp.bfloat16)
        second_normed = (normed_hat * second_gain[layer_at] + second_bias[layer_at]).astype(jnp.bfloat16)
        projected = jnp.dot(first_normed.reshape(-1, D), attention_weight[layer_at], preferred_element_type=jnp.float32)
        projected = projected.reshape(SEQS, LEN, H, 3, HD)
        bias_parts = attention_bias[layer_at].reshape(H, 2, HD)
        queries = rotate(projected[:, :, :, 0] + bias_parts[:, 0], cosine_table, sine_table).astype(jnp.bfloat16)
        keys = rotate(projected[:, :, :, 1], cosine_table, sine_table).astype(jnp.bfloat16)
        values = (projected[:, :, :, 2] + bias_parts[:, 1]).astype(jnp.bfloat16)
        mixed, totals = lax.map(forward_one, (queries, keys, values, segments))
        attended = jnp.dot(mixed.reshape(-1, D), project_weight[layer_at], preferred_element_type=jnp.float32)
        hidden = jnp.dot(second_normed.reshape(-1, D), expand_weight[layer_at], preferred_element_type=jnp.float32) + expand_bias[layer_at]
        activated = gelu_value(hidden).astype(jnp.bfloat16)
        expanded = jnp.dot(activated, contract_weight[layer_at], preferred_element_type=jnp.float32)
        stream = stream + (attended + expanded).reshape(SEQS, LEN, D) + project_bias[layer_at] + contract_bias[layer_at]
        saved.append((normed_hat, inv_std, first_normed, second_normed, queries, keys, values, mixed, totals, hidden))
    result = stream
    upstream = cotangent
    grads_by_name = {}
    for label in ['first_gain', 'first_bias', 'second_gain', 'second_bias', 'attention_weight', 'attention_bias', 'project_weight', 'project_bias', 'expand_weight', 'expand_bias', 'contract_weight']:
        grads_by_name[label] = [None] * LAYERS
    for layer_at in reversed(range(LAYERS)):
        normed_hat, inv_std, first_normed, second_normed, queries, keys, values, mixed, totals, hidden = saved[layer_at]
        upstream_flat = upstream.reshape(-1, D)
        upstream_half = upstream_flat.astype(jnp.bfloat16)
        grads_by_name['project_bias'][layer_at] = lax.optimization_barrier(jnp.sum(upstream_flat, axis=0))
        activated = gelu_value(hidden).astype(jnp.bfloat16)
        grads_by_name['contract_weight'][layer_at] = jnp.dot(activated.T, upstream_half, preferred_element_type=jnp.float32)
        hidden_grad = jnp.dot(upstream_half, contract_weight[layer_at].T, preferred_element_type=jnp.float32) * gelu_slope(hidden)
        hidden_half = hidden_grad.astype(jnp.bfloat16)
        grads_by_name['expand_weight'][layer_at] = jnp.dot(second_normed.reshape(-1, D).T, hidden_half, preferred_element_type=jnp.float32)
        grads_by_name['expand_bias'][layer_at] = lax.optimization_barrier(jnp.sum(hidden_grad, axis=0))
        second_grad = jnp.dot(hidden_half, expand_weight[layer_at].T, preferred_element_type=jnp.float32).reshape(SEQS, LEN, D)
        grads_by_name['project_weight'][layer_at] = jnp.dot(mixed.reshape(-1, D).T, upstream_half, preferred_element_type=jnp.float32)
        mixed_grad = jnp.dot(upstream_half, project_weight[layer_at].T, preferred_element_type=jnp.float32).astype(jnp.bfloat16)
        mixed_grad = mixed_grad.reshape(SEQS, LEN, H, HD)
        query_grad, key_grad, value_grad = lax.map(backward_one, (queries, keys, values, mixed, mixed_grad, totals, segments))
        query_grad = unrotate(query_grad, cosine_table, sine_table)
        key_grad = unrotate(key_grad, cosine_table, sine_table)
        grads_by_name['attention_bias'][layer_at] = jnp.stack([lax.optimization_barrier(jnp.sum(query_grad, axis=(0, 1))), lax.optimization_barrier(jnp.sum(value_grad, axis=(0, 1)))], axis=1).reshape(2 * D)
        projected_grad = jnp.stack([query_grad, key_grad, value_grad], axis=3).astype(jnp.bfloat16).reshape(-1, 3 * D)
        grads_by_name['attention_weight'][layer_at] = jnp.dot(first_normed.reshape(-1, D).T, projected_grad, preferred_element_type=jnp.float32)
        first_grad = jnp.dot(projected_grad, attention_weight[layer_at].T, preferred_element_type=jnp.float32).reshape(SEQS, LEN, D)
        grads_by_name['first_gain'][layer_at] = lax.optimization_barrier(jnp.sum(first_grad * normed_hat, axis=(0, 1)))
        grads_by_name['first_bias'][layer_at] = lax.optimization_barrier(jnp.sum(first_grad, axis=(0, 1)))
        grads_by_name['second_gain'][layer_at] = lax.optimization_barrier(jnp.sum(second_grad * normed_hat, axis=(0, 1)))
        grads_by_name['second_bias'][layer_at] = lax.optimization_barrier(jnp.sum(second_grad, axis=(0, 1)))
        hat_grad = first_grad * first_gain[layer_at] + second_grad * second_gain[layer_at]
        input_part = inv_std * (hat_grad - lax.optimization_barrier(jnp.mean(hat_grad, axis=-1, keepdims=True)) - normed_hat * lax.optimization_barrier(jnp.mean(hat_grad * normed_hat, axis=-1, keepdims=True)))
        upstream = upstream + input_part
    stacked = {}
    for label in grads_by_name:
        stacked[label] = jnp.stack(grads_by_name[label])
    return (result, upstream, stacked['first_gain'], stacked['first_bias'], stacked['second_gain'], stacked['second_bias'], stacked['attention_weight'], stacked['attention_bias'], stacked['project_weight'], stacked['project_bias'], stacked['expand_weight'], stacked['expand_bias'], stacked['contract_weight'], stacked['project_bias'])
```

```python
import jax
import jax.numpy as jnp
from jax import lax
from jax.experimental import pallas as pl
from jax.experimental.pallas import tpu as pltpu
from jax.sharding import PartitionSpec as P

HD = 64
ROT = 16
LAYERS = 2
MESH = pl.DeviceIdType.MESH
BF = jnp.bfloat16
F32 = jnp.float32

epsilon = 1e-05
root_half = 0.7071067811865476
gauss_norm = 0.3989422804014327
masked_score = -1e30

QKV, EXP, MIX, ALL = 384, 896, 896, 1536
NT = (((1,), (1,)), ((), ()))
TN = (((0,), (0,)), ((), ()))
VMEM_LIMIT = 62 * 1024 * 1024
WINDOW = 640


def dot(a, b, dims=(((1,), (0,)), ((), ()))):
    return lax.dot_general(a, b, dims, preferred_element_type=F32)


def place(i, r, sign):
    outer, inner = lax.div(i, 4), lax.rem(i, 4)
    r_outer, r_inner = (r // 4, r % 4) if isinstance(r, int) else (lax.div(r, 4), lax.rem(r, 4))
    return lax.rem(outer + r_outer, 2) * 4 + lax.rem(inner + 4 + sign * r_inner, 4)


def rows_of(i, count):
    return pl.ds(pl.multiple_of(i * count, count), count)


def remote(src, dst, send_sem, recv_sem, device):
    return pltpu.make_async_remote_copy(
        src_ref=src,
        dst_ref=dst,
        send_sem=send_sem,
        recv_sem=recv_sem,
        device_id=device,
        device_id_type=MESH,
    )


def meet(devices):
    barrier = pltpu.get_barrier_semaphore()
    for device in devices:
        pl.semaphore_signal(barrier, inc=1, device_id=device, device_id_type=MESH)
    pl.semaphore_wait(barrier, len(devices))


def gelu_value(hidden):
    return 0.5 * hidden * (1.0 + lax.erf(hidden * root_half))


def gelu_both(hidden):
    half = 0.5 * (1.0 + lax.erf(hidden * root_half))
    return hidden * half, half + hidden * jnp.exp(-0.5 * hidden * hidden) * gauss_norm


def norm_parts(stream):
    centre = stream - jnp.mean(stream, axis=-1, keepdims=True)
    inv_std = lax.rsqrt(jnp.mean(centre * centre, axis=-1, keepdims=True) + epsilon)
    return centre * inv_std, inv_std


def mask_bias(seg_col, seg_row, ahead):
    shape = (seg_col.shape[0], seg_row.shape[1])
    key_place = lax.broadcasted_iota(jnp.int32, shape, 1)
    query_place = lax.broadcasted_iota(jnp.int32, shape, 0) + ahead
    keep = (seg_col == seg_row) & (key_place <= query_place)
    return jnp.where(keep, 0.0, masked_score)


def head_masks(rows):
    lane = lax.broadcasted_iota(jnp.int32, (rows, 2 * HD), 1)
    return lane < HD


def pick(first_head, value, head):
    zero = jnp.zeros_like(value)
    return jnp.where(first_head, value, zero) if head == 0 else jnp.where(first_head, zero, value)


def lookup(i, table):
    found = table[0]
    for k in range(1, len(table)):
        found = jnp.where(i == k, table[k], found)
    return found


class Gather:
    order = (0, 3, 1, 4, 2, 5, 7, 6)

    def __init__(self, dp, t, ref, send, recv):
        self.t, self.ref, self.s, self.r = t, ref, send, recv
        self.up, self.down, self.over = ((dp, place(t, r, 1)) for r in (1, 3, 4))

    def peers(self):
        return [self.up, self.down, self.over]

    def rows(self, r, half=None):
        first = place(self.t, r, 1) * 128
        if half is None:
            return pl.ds(pl.multiple_of(first, 128), 128)
        return pl.ds(pl.multiple_of(first + half * 64, 64), 64)

    def copy(self, k, r, half, device):
        part = self.ref.at[self.rows(r, half), :]
        return remote(part, part, self.s.at[k], self.r.at[k], device)

    def sends(self):
        return (
            (0, 0, None, self.up), (1, 0, None, self.down), (2, 0, None, self.over),
            (3, 3, 0, self.up), (4, 1, 1, self.down),
            (5, 4, None, self.up), (6, 4, None, self.down), (7, 2, None, self.over),
        )

    def send(self, k):
        self.copy(*self.sends()[k]).start()

    def came(self, k):
        r, half = ((3, None), (1, None), (4, None), (2, 0), (2, 1), (7, None), (5, None), (6, None))[k]
        self.copy(k, r, half, self.up).wait_recv()

    def begin(self):
        for k in range(3):
            self.send(k)

    def relay_one(self):
        self.came(0)
        self.send(3)
        self.came(1)
        self.send(4)
        self.came(2)
        self.send(5)
        self.send(6)

    def relay_two(self):
        self.came(3)
        self.came(4)
        self.send(7)

    def before(self, i):
        pl.when(i == 1)(self.relay_one)
        pl.when(i == 4)(self.relay_two)
        self.late(i)

    def late(self, i):
        @pl.when(i == 5)
        def _():
            self.came(5)
            self.came(6)

        pl.when(i == 7)(lambda: self.came(7))

    def end(self):
        for k in range(8):
            self.copy(*self.sends()[k]).wait_send()


class Scatter:
    order = (6, 5, 7, 2, 4, 1, 3, 0)

    def __init__(self, dp, t, part, got, total, send, recv):
        self.part, self.got, self.total, self.s, self.r = part, got, total, send, recv
        self.up, self.down, self.over = ((dp, place(t, r, 1)) for r in (1, 3, 4))

    def copy(self, k):
        slot, first, count, device = (
            (0, 0, 128, self.over), (1, 0, 128, self.up), (2, 0, 128, self.down),
            (3, 0, 64, self.up), (3, 64, 64, self.down),
            (4, 0, 128, self.over), (5, 0, 128, self.up), (6, 0, 128, self.down),
        )[k]
        return remote(
            self.part.at[slot * 128 + first : slot * 128 + first + count, :],
            self.got.at[k * 128 : k * 128 + count, :],
            self.s.at[k], self.r.at[k], device,
        )

    def add(self, k, first=0, count=128):
        self.copy(k).wait_recv()
        self.total[first : first + count, :] += self.got[k * 128 : k * 128 + count, :].astype(F32)

    def step(self, j, partial):
        self.total[...] = partial

        @pl.when(j == 3)
        def _():
            self.add(0)

        @pl.when(j == 4)
        def _():
            self.add(1)
            self.add(2)

        @pl.when(j == 5)
        def _():
            self.add(3, 0, 64)

        @pl.when(j == 6)
        def _():
            self.add(4, 64, 64)

        @pl.when(j < 7)
        def _():
            self.part[rows_of(j, 128), :] = self.total[...].astype(BF)

        for at, ks in ((0, (0,)), (1, (1,)), (2, (2,)), (3, (3, 4)), (4, (5,)), (5, (6,)), (6, (7,))):

            @pl.when(j == at)
            def _(ks=ks):
                for k in ks:
                    self.copy(k).start()

    def sum(self):
        for k in (5, 6, 7):
            self.add(k)
        return self.total[...]

    def end(self):
        for k in range(8):
            self.copy(k).wait_send()


class WeightGather:
    def __init__(self, dp, t, src, target, columns, send, recv, hand_send, hand_recv):
        self.chip, self.core = lax.div(dp, 2), lax.rem(dp, 2)
        self.src, self.ref, self.columns = src.at[:, columns], target, columns
        self.s, self.r, self.hs, self.hr = send, recv, hand_send, hand_recv
        self.up, self.down, self.over = ((place(self.chip, r, 1) * 2 + self.core, t) for r in (1, 3, 4))
        self.sibling = (self.chip * 2 + 1 - self.core, t)

    def peers(self):
        return [self.up, self.down, self.over, self.sibling]

    def rows(self, r, half=None, other=False):
        core = 1 - self.core if other else self.core
        first = (place(self.chip, r, 1) * 2 + core) * 64
        if half is None:
            return pl.ds(pl.multiple_of(first, 64), 64)
        return pl.ds(pl.multiple_of(first + half * 32, 32), 32)

    def copy(self, k, r, half, device):
        part = self.ref.at[self.rows(r, half), self.columns]
        return remote(part if r else self.src, part, self.s.at[k], self.r.at[k], device)

    def sends(self):
        return (
            (0, 0, None, self.up), (1, 0, None, self.down), (2, 0, None, self.over),
            (3, 3, 0, self.up), (4, 1, 1, self.down),
            (5, 4, None, self.up), (6, 4, None, self.down),
            (7, 7, 0, self.up), (8, 5, 1, self.down),
        )

    def send(self, k):
        self.copy(*self.sends()[k]).start()

    def came(self, k):
        r, half = ((3, None), (1, None), (4, None), (2, 0), (2, 1), (7, None), (5, None), (6, 0), (6, 1))[k]
        self.copy(k, r, half, self.up).wait_recv()

    def hand(self, r):
        part = self.ref.at[self.rows(r), self.columns]
        return remote(part if r else self.src, part, self.hs.at[r], self.hr.at[r], self.sibling)

    def handed(self, r):
        part = self.ref.at[self.rows(r, None, True), self.columns]
        return remote(part, part, self.hs.at[r], self.hr.at[r], self.sibling)

    def begin(self):
        for k in range(3):
            self.send(k)
        self.hand(0).start()
        self.ref[self.rows(0), self.columns] = self.src[...]

    def relay_one(self):
        for k, r, onward in ((0, 3, (3,)), (1, 1, (4,)), (2, 4, (5, 6))):
            self.came(k)
            for m in onward:
                self.send(m)
            self.hand(r).start()

    def relay_two(self):
        self.came(3)
        self.came(4)
        self.hand(2).start()
        for k, r, onward in ((5, 7, 7), (6, 5, 8)):
            self.came(k)
            self.send(onward)
            self.hand(r).start()

    def relay_three(self):
        self.came(7)
        self.came(8)
        self.hand(6).start()

    def end(self):
        for r in range(8):
            self.handed(r).wait_recv()
            self.hand(r).wait_send()
        for k in range(9):
            self.copy(*self.sends()[k]).wait_send()


class GradSum:
    def __init__(self, dp, t, g_ref, out_ref, pair_ref, got_ref, p_send, p_recv, g_send, g_recv):
        self.chip, self.core = lax.div(dp, 2), lax.rem(dp, 2)
        self.up, self.down, self.over = ((place(self.chip, r, 1) * 2 + self.core, t) for r in (1, 3, 4))
        self.sibling = (self.chip * 2 + 1 - self.core, t)
        self.g, self.pair, self.got, self.out = g_ref, pair_ref, got_ref, out_ref
        self.p_send, self.p_recv, self.s, self.r = p_send, p_recv, g_send, g_recv

    def peers(self):
        return [self.up, self.down, self.over, self.sibling]

    def pair_copy(self):
        return remote(
            self.g.at[rows_of(1 - self.core, 512), :], self.pair, self.p_send.at[0], self.p_recv.at[0], self.sibling
        )

    def rows(self, r, half=None):
        first = place(self.chip, r, 1) * 64
        if half is None:
            return pl.ds(pl.multiple_of(first, 64), 64)
        return pl.ds(pl.multiple_of(first + half * 32, 32), 32)

    def copy(self, k):
        r, half, device = (
            (6, 0, self.up), (6, 1, self.down), (2, 0, self.up), (2, 1, self.down),
            (5, None, self.up), (7, None, self.down), (1, None, self.up), (3, None, self.down),
            (4, None, self.over),
        )[k]
        count = 64 if half is None else 32
        return remote(
            self.pair.at[self.rows(r, half), :],
            self.got.at[k * 64 : k * 64 + count, :],
            self.s.at[k], self.r.at[k], device,
        )

    def add(self, k, r, half=None):
        self.copy(k).wait_recv()
        count = 64 if half is None else 32
        rows = self.rows(r, half)
        arrived = self.got[k * 64 : k * 64 + count, :].astype(F32)
        self.pair[rows, :] = (self.pair[rows, :].astype(F32) + arrived).astype(BF)

    def begin(self):
        self.pair_copy().start()

    def one(self):
        self.pair_copy().wait()
        for r in (6, 2, 5, 7, 1, 3, 4, 0):
            rows = self.rows(r)
            own = self.g[rows_of(self.core * 8 + place(self.chip, r, 1), 64), :].astype(F32)
            both = self.pair[rows, :].astype(F32) + own
            if r:
                self.pair[rows, :] = both.astype(BF)
            else:
                self.out[...] = both
            for k in {6: (0, 1), 2: (2, 3)}.get(r, ()):
                self.copy(k).start()

    def two(self):
        for k, r, half in ((0, 5, 0), (1, 7, 1), (2, 1, 0), (3, 3, 1)):
            self.add(k, r, half)
            self.copy(k + 4).start()

    def three(self):
        self.add(4, 4)
        self.add(5, 4)
        self.copy(8).start()

    def end(self):
        for k in (6, 7, 8):
            self.copy(k).wait_recv()
            self.out[...] += self.got[k * 64 : (k + 1) * 64, :].astype(F32)
        for k in range(9):
            self.copy(k).wait_send()


class Bag:
    pass


def make_tables(seg_row_ref, m):
    seg = seg_row_ref[...].astype(F32)
    m.seg_row[...] = jnp.broadcast_to(seg, (8, 1024))
    first_place = jnp.zeros_like(seg)
    for value in range(3):
        count = jnp.sum((seg == value).astype(F32), axis=1, keepdims=True)
        first_place = first_place + jnp.where(seg > value, count, 0.0)
    offset = lax.broadcasted_iota(jnp.int32, (1, 1024), 1).astype(F32) - first_place
    which = lax.broadcasted_iota(jnp.int32, (8, 1), 0)
    frequency = lookup(which, [10000.0 ** (-2.0 * i / ROT) for i in range(ROT // 2)])
    angles = frequency * offset
    cosine, sine = jnp.cos(angles), jnp.sin(angles)
    lane = lax.broadcasted_iota(jnp.int32, (8, 128), 1)
    row = lax.broadcasted_iota(jnp.int32, (8, 128), 0)
    feature = lane & (HD - 1)
    same = (lane & 7) == row

    def spread(values, where, sign):
        choice = jnp.where(where, sign, 0.0)
        return lax.dot_general(values, choice, TN, preferred_element_type=F32, precision=lax.Precision.HIGHEST)

    still = ((lax.broadcasted_iota(jnp.int32, (1024, 128), 1) & (HD - 1)) >= ROT).astype(F32)
    m.cos[...] = spread(cosine, same & (feature < ROT), 1.0) + still
    m.sin1[...] = spread(sine, same & (feature < ROT // 2), -1.0)
    m.sin2[...] = spread(sine, same & (feature < ROT) & (feature >= ROT // 2), 1.0)
    m.seg_col[...] = spread(m.seg_row[...], row == 0, 1.0)


def window_of(c):
    return pl.multiple_of(lax.max(c - 4, 0) * 128, 128)


def window_bias(m, rows, c):
    start = window_of(c)
    return mask_bias(m.seg_col[rows, 0:1], m.seg_row[0:1, pl.ds(start, WINDOW)], c * 128 - start)


def rotate(x, m, rows):
    return (
        x * m.cos[rows, :]
        + pltpu.roll(x, 120, 1) * m.sin1[rows, :]
        + pltpu.roll(x, 8, 1) * m.sin2[rows, :]
    )


def unrotate(d, m, rows):
    return (
        d * m.cos[rows, :]
        - pltpu.roll(d, 120, 1) * m.sin1[rows, :]
        - pltpu.roll(d, 8, 1) * m.sin2[rows, :]
    )


def enter_forward(rows, vec, abias, ebias, m, L):
    hat = L.nhat[rows, :].astype(F32)
    one = (hat * vec[0:1, :] + vec[1:2, :]).astype(BF)
    two = (hat * vec[2:3, :] + vec[3:4, :]).astype(BF)
    projected = dot(one, L.w[:, :QKV]) + abias
    L.qkv[rows, 0:128] = (rotate(projected[:, 0:128], m, rows) * 0.125).astype(BF)
    L.qkv[rows, 128:256] = rotate(projected[:, 128:256], m, rows).astype(BF)
    L.qkv[rows, 256:384] = projected[:, 256:384].astype(BF)
    hidden = dot(two, L.w[:, QKV:EXP]) + ebias
    L.hidden[rows, :] = hidden
    L.ma[rows, 128:640] = gelu_value(hidden).astype(BF)


def attend_forward(c, rows, m, L):
    bias = window_bias(m, rows, c)
    keys_at = pl.ds(window_of(c), WINDOW)
    q = L.qkv[rows, 0:128]
    keys = L.qkv[keys_at, 128:256]
    values = L.qkv[keys_at, 256:384]
    first_head = head_masks(128)
    outs = []
    for head in range(2):
        scores = dot(pick(first_head, q, head), keys, NT) + bias
        row_max = jnp.max(scores, axis=-1, keepdims=True)
        exps = jnp.exp(scores - row_max)
        row_sum = jnp.sum(exps, axis=-1, keepdims=True)
        L.lse[rows, head : head + 1] = row_max + jnp.log(row_sum)
        outs.append(dot((exps * (1.0 / row_sum)).astype(BF), values))
    L.ma[rows, 0:128] = jnp.where(first_head, outs[0], outs[1]).astype(BF)


def enter_backward(rows, layer, m, L):
    back = dot(L.up_all[rows, :], L.w[:, MIX:ALL])
    m.mg[rows, :] = back[:, 0:128].astype(BF)
    _, slope = gelu_both(L.hidden[rows, :])
    hidden_grad = back[:, 128:640] * slope
    m.biases[layer : layer + 1, 256:768] += jnp.sum(hidden_grad, axis=0, keepdims=True)
    m.hh[rows, :] = hidden_grad.astype(BF)


def attend_backward(c, layer, m, L):
    rows = rows_of(c, 128)
    bias = window_bias(m, rows, c)
    keys_at = pl.ds(window_of(c), WINDOW)
    q = L.qkv[rows, 0:128]
    keys = L.qkv[keys_at, 128:256]
    values = L.qkv[keys_at, 256:384]
    out_grad = m.mg[rows, :]
    product = out_grad.astype(F32) * L.ma[rows, 0:128].astype(F32)
    first_head = head_masks(128)
    query_grads, key_grads, value_grads = [], [], []
    for head in range(2):
        scores = dot(pick(first_head, q, head), keys, NT) + bias
        soft = jnp.exp(scores - L.lse[rows, head : head + 1])
        prob_grad = dot(pick(first_head, out_grad, head), values, NT)
        delta = jnp.sum(pick(first_head, product, head), axis=-1, keepdims=True)
        score_grad = (soft * (prob_grad - delta)).astype(BF)
        query_grads.append(dot(score_grad, keys))
        key_grads.append(dot(score_grad, q, TN))
        value_grads.append(dot(soft.astype(BF), out_grad, TN))
    wide_first = head_masks(WINDOW)
    m.dk[keys_at, :] += jnp.where(wide_first, key_grads[0], key_grads[1])
    m.dv[keys_at, :] += jnp.where(wide_first, value_grads[0], value_grads[1])
    query_grad = unrotate(jnp.where(first_head, query_grads[0], query_grads[1]) * 0.125, m, rows)
    m.biases[layer : layer + 1, 0:128] += jnp.sum(query_grad, axis=0, keepdims=True)
    m.pg[rows, 0:128] = query_grad.astype(BF)


def close_attention(c, layer, m):
    rows = rows_of(c, 128)
    m.pg[rows, 128:256] = unrotate(m.dk[rows, :], m, rows).astype(BF)
    value_grad = m.dv[rows, :]
    m.biases[layer : layer + 1, 128:256] += jnp.sum(value_grad, axis=0, keepdims=True)
    m.pg[rows, 256:384] = value_grad.astype(BF)


def leave_backward(rows, layer, vec, m, L):
    first_grad = dot(m.pg[rows, :], L.w[:, :QKV], NT)
    second_grad = dot(m.hh[rows, :], L.w[:, QKV:EXP], NT)
    hat = L.nhat[rows, :].astype(F32)
    for k, value in enumerate((first_grad * hat, first_grad, second_grad * hat, second_grad)):
        at = 5 * layer + k
        m.small[at : at + 1, :] += jnp.sum(value, axis=0, keepdims=True)
    return first_grad * vec[0:1, :] + second_grad * vec[2:3, :]


def put_by_owner(target, i, value, columns):
    target[rows_of(i, 64), columns] = value[0:64].astype(BF)
    target[rows_of(i + 8, 64), columns] = value[64:128].astype(BF)


def weight_grads(kind, vec, m, L):
    def step(i, carry):
        at = pl.ds(pl.multiple_of(i * 128, 128), 128)
        if kind == "out":
            put_by_owner(L.g_ff, i, dot(L.up_all[:, at], L.ma[...], TN), slice(512, 1152))
        else:
            k = 0 if kind == "in" else 2
            normed = (L.nhat[:, at].astype(F32) * vec[k : k + 1, at] + vec[k + 1 : k + 2, at]).astype(BF)
            if kind == "in":
                put_by_owner(L.g_in, i, dot(normed, m.pg[...], TN), slice(0, 384))
            else:
                put_by_owner(L.g_ff, i, dot(normed, m.hh[...], TN), slice(0, 512))
        return carry

    lax.fori_loop(0, 8, step, 0)


class Sums:
    def __init__(self, dp, t, m):
        self.dp, self.t, self.m = dp, t, m

    def tensor_peer(self, r):
        return (self.dp, place(self.t, r, 1))

    def dp_peer(self, r):
        return (lax.rem(self.dp + r, 16), self.t)

    def peers(self):
        return [self.tensor_peer(r) for r in range(1, 8)] + [self.dp_peer(r) for r in range(1, 16)]

    def lanes(self, i):
        return pl.ds(pl.multiple_of(i * 128, 128), 128)

    def bias_copy(self, r, came=False):
        m = self.m
        at = rows_of(lax.rem(self.dp + 16 - r, 16), 8) if came else rows_of(self.dp, 8)
        src = m.all_biases.at[at, :] if came else m.biases
        return remote(src, m.all_biases.at[at, :], m.e_send.at[r], m.e_recv.at[r], self.dp_peer(r))

    def t_copy(self, r, came=False):
        m, to = self.m, place(self.t, r, 1)
        at = rows_of(place(self.t, r, -1), 16) if came else rows_of(self.t, 16)
        return remote(m.small.at[:, self.lanes(to)], m.t_all.at[at, :], m.t_send.at[r], m.t_recv.at[r], self.tensor_peer(r))

    def d_copy(self, r, came=False):
        m = self.m
        at = rows_of(lax.rem(self.dp + 16 - r, 16), 16) if came else rows_of(self.dp, 16)
        return remote(m.d_all.at[at, :], m.d_all.at[at, :], m.d_send.at[r], m.d_recv.at[r], self.dp_peer(r))

    def u_copy(self, r, came=False):
        m = self.m
        at = self.lanes(place(self.t, r, -1) if came else self.t)
        return remote(m.total.at[:, at], m.total.at[:, at], m.u_send.at[r], m.u_recv.at[r], self.tensor_peer(r))

    def send_biases(self):
        self.m.all_biases[rows_of(self.dp, 8), :] = self.m.biases[...]
        for r in range(1, 16):
            self.bias_copy(r).start()

    def begin(self):
        self.m.t_all[rows_of(self.t, 16), :] = self.m.small[:, self.lanes(self.t)]
        for r in range(1, 8):
            self.t_copy(r).start()

    def over_dp(self):
        m = self.m
        for r in range(1, 8):
            self.t_copy(r, True).wait_recv()
        total = m.t_all[0:16, :]
        for i in range(1, 8):
            total = total + m.t_all[i * 16 : (i + 1) * 16, :]
        m.d_all[rows_of(self.dp, 16), :] = total
        for r in range(1, 16):
            self.d_copy(r).start()

    def back(self):
        m = self.m
        for r in range(1, 16):
            self.d_copy(r, True).wait_recv()
        total = m.d_all[0:16, :]
        for i in range(1, 16):
            total = total + m.d_all[i * 16 : (i + 1) * 16, :]
        m.total[:, self.lanes(self.t)] = total
        for r in range(1, 8):
            self.u_copy(r).start()

    def end(self):
        m = self.m
        for r in range(1, 16):
            self.bias_copy(r, True).wait_recv()
        total = m.all_biases[0:8, :]
        for i in range(1, 16):
            total = total + m.all_biases[i * 8 : (i + 1) * 8, :]
        m.bias_total[...] = total
        for r in range(1, 8):
            self.u_copy(r, True).wait_recv()
        for r in range(1, 8):
            self.t_copy(r).wait_send()
            self.u_copy(r).wait_send()
        for r in range(1, 16):
            self.d_copy(r).wait_send()
            self.bias_copy(r).wait_send()


INPUTS = (
    ("residual", (128, 1024), BF),
    ("seg_in", (1, 1024), jnp.int32),
    ("gain1", (2, 1024), F32),
    ("bias1", (2, 1024), F32),
    ("gain2", (2, 1024), F32),
    ("bias2", (2, 1024), F32),
    ("attention_weight", (2, 64, 384), BF),
    ("attention_bias", (2, 256), F32),
    ("project_weight", (2, 128, 64), BF),
    ("project_bias", (2, 1024), F32),
    ("expand_weight", (2, 64, 512), BF),
    ("ebias", (2, 512), F32),
    ("contract_weight", (2, 512, 64), BF),
    ("contract_bias", (2, 1024), F32),
    ("cotangent", (128, 1024), F32),
)
OUTPUTS = (
    ("result", (128, 1024), F32),
    ("residual_grad", (128, 1024), F32),
    ("ff_sum0", (64, 1152), F32),
    ("in_sum0", (64, 384), F32),
    ("ff_sum1", (64, 1152), F32),
    ("in_sum1", (64, 384), F32),
    ("total", (16, 1024), F32),
    ("bias_total", (8, 768), F32),
)


def dma(*shape):
    return pltpu.SemaphoreType.DMA(shape)


def scratch():
    vmem = pltpu.VMEM
    found = [(name, vmem(shape, dtype)) for name, shape, dtype in INPUTS] + [
        ("in_sems", dma(len(INPUTS))),
        ("packed", vmem((2, 64, ALL), BF)),
        ("vec", vmem((2, 8, 1024), F32)),
        ("abias", vmem((2, 384), F32)),
        ("seg_row", vmem((8, 1024), F32)),
        ("cos", vmem((1024, 128), F32)),
        ("sin1", vmem((1024, 128), F32)),
        ("sin2", vmem((1024, 128), F32)),
        ("seg_col", vmem((1024, 128), F32)),
        ("stream", vmem((128, 1024), F32)),
        ("up", vmem((128, 1024), F32)),
        ("part", vmem((1024, 1024), BF)),
        ("sum", vmem((128, 1024), F32)),
        ("mg", vmem((1024, 128), BF)),
        ("hh", vmem((1024, 512), BF)),
        ("pg", vmem((1024, 384), BF)),
        ("dk", vmem((1024, 128), F32)),
        ("dv", vmem((1024, 128), F32)),
        ("small", vmem((16, 1024), F32)),
        ("biases", vmem((8, 768), F32)),
        ("all_biases", vmem((128, 768), F32)),
        ("t_all", vmem((128, 128), F32)),
        ("d_all", vmem((256, 128), F32)),
        ("e_send", dma(16)), ("e_recv", dma(16)),
        ("t_send", dma(8)), ("t_recv", dma(8)),
        ("d_send", dma(16)), ("d_recv", dma(16)),
        ("u_send", dma(8)), ("u_recv", dma(8)),
        ("ag_send", dma(4, 8)), ("ag_recv", dma(4, 8)),
        ("rs_send", dma(4, 8)), ("rs_recv", dma(4, 8)),
        ("w_send", dma(3, 9)), ("w_recv", dma(3, 9)),
        ("wh_send", dma(3, 8)), ("wh_recv", dma(3, 8)),
        ("p_send", dma(4, 1)), ("p_recv", dma(4, 1)),
        ("g_send", dma(4, 9)), ("g_recv", dma(4, 9)),
    ]
    for layer in range(LAYERS):
        found += [
            (f"{name}{layer}", vmem(shape, dtype))
            for name, shape, dtype in (
                ("w", (1024, ALL), BF),
                ("nhat", (1024, 1024), BF),
                ("up_all", (1024, 1024), BF),
                ("qkv", (1024, 384), BF),
                ("ma", (1024, 640), BF),
                ("hidden", (1024, 512), F32),
                ("lse", (1024, 2), F32),
                ("got_f", (1024, 1024), BF),
                ("got_b", (1024, 1024), BF),
                ("g_ff", (1024, 1152), BF),
                ("g_in", (1024, 384), BF),
                ("pair_ff", (512, 1152), BF),
                ("pair_in", (512, 384), BF),
                ("got_ff", (576, 1152), BF),
                ("got_in", (576, 384), BF),
            )
        ]
    return found


def by_part(columns):
    return jnp.concatenate([columns[:, k * HD : (k + 1) * HD] for k in (0, 3, 1, 4, 2, 5)], axis=1)


def by_head(columns):
    return jnp.concatenate([columns[:, k * HD : (k + 1) * HD] for k in (0, 2, 4, 1, 3, 5)], axis=1)


def pack(m):
    for layer in range(LAYERS):
        m.packed[layer, :, 0:384] = by_part(m.attention_weight[layer])
        m.packed[layer, :, 384:896] = m.expand_weight[layer]
        m.packed[layer, :, 896:1024] = m.project_weight[layer].T
        m.packed[layer, :, 1024:1536] = m.contract_weight[layer].T


def whole_kernel(*refs):
    m = Bag()
    taken = [name for name, _, _ in INPUTS]
    names = [f"far_{name}" for name in taken] + [o[0] for o in OUTPUTS] + [k for k, _ in scratch()]
    for name, ref in zip(names, refs, strict=True):
        setattr(m, name, ref)

    def fetch(name):
        far = getattr(m, f"far_{name}")
        near = getattr(m, name)
        far = far if far.shape == near.shape else far.at[0]
        return pltpu.make_async_copy(far, near, m.in_sems.at[taken.index(name)])

    early = ["attention_weight", "project_weight", "expand_weight", "contract_weight", "residual"]
    later = [name for name in taken if name not in early]
    for name in early + later:
        fetch(name).start()
    layers = []
    for layer in range(LAYERS):
        L = Bag()
        for name in ("w", "nhat", "up_all", "qkv", "ma", "hidden", "lse", "g_ff", "g_in"):
            setattr(L, name, getattr(m, f"{name}{layer}"))
        L.vec = m.vec.at[layer]
        L.abias = m.abias.at[layer : layer + 1, :]
        L.ebias = m.ebias.at[layer : layer + 1, :]
        layers.append(L)
    first, second = layers
    dp, t = lax.axis_index("dp"), lax.axis_index("tensor")

    def gather(k, ref):
        return Gather(dp, t, ref, m.ag_send.at[k], m.ag_recv.at[k])

    def scatter(k, got):
        return Scatter(dp, t, m.part, got, m.sum, m.rs_send.at[k], m.rs_recv.at[k])

    def grad_sum(k, g, out, pair, got):
        return GradSum(dp, t, g, out, pair, got, m.p_send.at[k], m.p_recv.at[k], m.g_send.at[k], m.g_recv.at[k])

    parts = ((0, slice(0, EXP)), (0, slice(EXP, ALL)), (1, slice(0, ALL)))
    weights = [
        WeightGather(
            dp, t, m.packed.at[layer], layers[layer].w, columns,
            m.w_send.at[k], m.w_recv.at[k], m.wh_send.at[k], m.wh_recv.at[k],
        )
        for k, (layer, columns) in enumerate(parts)
    ]
    hats = [gather(k, layers[k].nhat) for k in range(2)]
    ups = [gather(2 + k, layers[k].up_all) for k in range(2)]
    outs = [scatter(0, m.got_f0), scatter(1, m.got_f1)]
    backs = [scatter(2, m.got_b0), scatter(3, m.got_b1)]
    ff = [
        grad_sum(0, m.g_ff0, m.ff_sum0, m.pair_ff0, m.got_ff0),
        grad_sum(1, m.g_ff1, m.ff_sum1, m.pair_ff1, m.got_ff1),
    ]
    inn = [
        grad_sum(2, m.g_in0, m.in_sum0, m.pair_in0, m.got_in0),
        grad_sum(3, m.g_in1, m.in_sum1, m.pair_in1, m.got_in1),
    ]
    sums = Sums(dp, t, m)
    for name in early:
        fetch(name).wait()
    pack(m)
    meet(sums.peers())

    def at_block(table, j):
        c = place(t, lookup(j, table), 1)
        return c, rows_of(c, 128)

    weights[0].begin()
    stream0 = m.residual[...].astype(F32)
    mine = rows_of(t, 128)
    first.nhat[mine, :] = norm_parts(stream0)[0].astype(BF)
    hats[0].begin()
    for name in later:
        fetch(name).wait()
    second.up_all[mine, :] = m.cotangent[...].astype(BF)
    m.small[...] = jnp.zeros_like(m.small)
    m.biases[...] = jnp.zeros_like(m.biases)
    m.vec[...] = jnp.zeros_like(m.vec)
    for k, value in enumerate((m.gain1, m.bias1, m.gain2, m.bias2)):
        for layer in range(LAYERS):
            m.vec[layer, k : k + 1, :] = value[layer : layer + 1, :]
    for layer in range(LAYERS):
        m.vec[layer, 4:5, :] = m.project_bias[layer : layer + 1, :] + m.contract_bias[layer : layer + 1, :]
    pairs = m.attention_bias[...]
    m.abias[:, 0:128] = jnp.concatenate([pairs[:, 0:64], pairs[:, 128:192]], axis=1)
    m.abias[:, 128:256] = jnp.zeros((2, 128), F32)
    m.abias[:, 256:384] = jnp.concatenate([pairs[:, 64:128], pairs[:, 192:256]], axis=1)
    make_tables(m.seg_in, m)
    weights[0].relay_one()
    hats[0].relay_one()
    weights[1].begin()
    weights[0].relay_two()
    hats[0].relay_two()
    ups[1].begin()
    weights[0].relay_three()
    weights[0].end()
    weights[1].relay_one()

    def enter0(i, carry):
        hats[0].late(i)
        enter_forward(at_block(Gather.order, i)[1], first.vec, first.abias[...], first.ebias[...], m, first)
        pl.when(i == 4)(weights[1].relay_two)
        return carry

    lax.fori_loop(0, 8, enter0, 0)
    ups[1].relay_one()
    weights[1].relay_three()
    weights[1].end()
    weights[2].begin()

    def attend0(j, carry):
        c, rows = at_block(Scatter.order, j)
        attend_forward(c, rows, m, first)
        outs[0].step(j, dot(first.ma[rows, :], first.w[:, MIX:ALL], NT))
        pl.when(j == 3)(weights[2].relay_one)
        pl.when(j == 4)(ups[1].relay_two)
        pl.when(j == 6)(weights[2].relay_two)
        return carry

    lax.fori_loop(0, 8, attend0, 0)
    stream1 = outs[0].sum() + m.residual[...].astype(F32) + first.vec[4:5, :]
    m.stream[...] = stream1

    second.nhat[mine, :] = norm_parts(stream1)[0].astype(BF)
    hats[1].begin()
    weights[2].relay_three()
    outs[0].end()
    weights[2].end()

    def enter1(i, carry):
        hats[1].before(i)
        enter_forward(at_block(Gather.order, i)[1], second.vec, second.abias[...], second.ebias[...], m, second)
        return carry

    lax.fori_loop(0, 8, enter1, 0)

    def attend1(j, carry):
        c, rows = at_block(Scatter.order, j)
        attend_forward(c, rows, m, second)
        outs[1].step(j, dot(second.ma[rows, :], second.w[:, MIX:ALL], NT))
        return carry

    lax.fori_loop(0, 8, attend1, 0)

    def back_through(layer, L, start, early, middle, late):
        m.dk[...] = jnp.zeros_like(m.dk)
        m.dv[...] = jnp.zeros_like(m.dv)

        def enter(i, carry):
            if layer == 0:
                ups[0].late(i)
            enter_backward(at_block(Gather.order, i)[1], layer, m, L)
            return carry

        lax.fori_loop(0, 8, enter, 0)
        start()

        def attend(c, carry):
            attend_backward(c, layer, m, L)
            early(c)
            return carry

        lax.fori_loop(0, 8, attend, 0)

        def close(c, carry):
            close_attention(c, layer, m)
            return carry

        lax.fori_loop(0, 8, close, 0)
        middle()

        def leave(j, carry):
            rows = at_block(Scatter.order, j)[1]
            backs[layer].step(j, leave_backward(rows, layer, L.vec, m, L))
            late(j)
            return carry

        lax.fori_loop(0, 8, leave, 0)

    def to_stream(layer, up, stream):
        hat_grad = backs[layer].sum()
        hat, inv_std = norm_parts(stream)
        return up + inv_std * (
            hat_grad
            - jnp.mean(hat_grad, axis=-1, keepdims=True)
            - hat * jnp.mean(hat_grad * hat, axis=-1, keepdims=True)
        )

    def nothing(*_):
        pass

    ups[1].came(5)
    ups[1].came(6)
    ups[1].came(7)
    m.small[9:10, :] = jnp.sum(m.cotangent[...], axis=0, keepdims=True)

    def result():
        m.result[...] = outs[1].sum() + m.stream[...] + second.vec[4:5, :]
        outs[1].end()

    def late1(j):
        pl.when(j == 2)(lambda: weight_grads("out", second.vec, m, second))

    back_through(1, second, result, nothing, nothing, late1)
    up = to_stream(1, m.cotangent[...], m.stream[...])
    m.up[...] = up
    first.up_all[mine, :] = up.astype(BF)
    ups[0].begin()
    m.small[4:5, :] = jnp.sum(up, axis=0, keepdims=True)
    weight_grads("expand", second.vec, m, second)
    ff[1].begin()
    backs[1].end()
    ups[0].relay_one()
    weight_grads("in", second.vec, m, second)
    inn[1].begin()
    ff[1].one()
    ups[0].relay_two()
    inn[1].one()

    def start0():
        ff[1].two()
        inn[1].two()
        weight_grads("out", first.vec, m, first)
        weight_grads("expand", first.vec, m, first)
        ff[0].begin()

    def early0(c):
        @pl.when(c == 2)
        def _():
            ff[1].three()
            inn[1].three()
            ff[0].one()

        pl.when(c == 6)(ff[0].two)

    def late0(j):
        @pl.when(j == 2)
        def _():
            weight_grads("in", first.vec, m, first)
            inn[0].begin()

        pl.when(j == 3)(ff[0].three)
        pl.when(j == 5)(inn[0].one)

    back_through(0, first, start0, early0, sums.send_biases, late0)
    sums.begin()
    inn[0].two()
    ff[1].end()
    inn[1].end()
    sums.over_dp()
    m.residual_grad[...] = to_stream(0, m.up[...], m.residual[...].astype(F32))
    inn[0].three()
    sums.back()
    ff[0].end()
    inn[0].end()
    sums.end()
    backs[0].end()
    for each in hats + ups:
        each.end()


def outputs_kernel(
    result, residual_grad, ff0, in0, ff1, in1, total, bias_total,
    result_out, residual_grad_out, gain1, bias1, gain2, bias2,
    attention_weight, attention_bias, project_weight, project_bias, expand_weight, expand_bias, contract_weight, contract_bias,
):
    result_out[0] = result[...]
    residual_grad_out[0] = residual_grad[...]
    for layer, (ff, inn) in enumerate(((ff0, in0), (ff1, in1))):
        for k, out in enumerate((gain1, bias1, gain2, bias2, project_bias)):
            out[layer : layer + 1, :] = total[5 * layer + k : 5 * layer + k + 1, :]
        contract_bias[layer : layer + 1, :] = total[5 * layer + 4 : 5 * layer + 5, :]
        attention_weight[layer] = by_head(inn[...])
        expand_weight[layer] = ff[:, 0:512]
        project_weight[layer] = ff[:, 512:640].T
        contract_weight[layer] = ff[:, 640:1152].T
    biases = bias_total[0:2, :]
    attention_bias[...] = jnp.concatenate(
        [biases[:, k * HD : (k + 1) * HD] for k in (0, 2, 1, 3)], axis=1
    )
    expand_bias[...] = biases[:, 256:768]


def body(
    residual,
    segments,
    first_gain,
    first_bias,
    second_gain,
    second_bias,
    attention_weight,
    attention_bias,
    project_weight,
    project_bias,
    expand_weight,
    expand_bias,
    contract_weight,
    contract_bias,
    cotangent,
):
    args = (
        residual,
        segments,
        first_gain,
        first_bias,
        second_gain,
        second_bias,
        attention_weight,
        attention_bias,
        project_weight,
        project_bias,
        expand_weight,
        expand_bias,
        contract_weight,
        contract_bias,
        cotangent,
    )
    vmem = pl.BlockSpec(memory_space=pltpu.VMEM)
    found = pl.pallas_call(
        whole_kernel,
        name="layers",
        out_shape=[jax.ShapeDtypeStruct(shape, dtype) for _, shape, dtype in OUTPUTS],
        in_specs=[pl.BlockSpec(memory_space=pl.ANY)] * len(args),
        out_specs=[vmem] * len(OUTPUTS),
        scratch_shapes=[spec for _, spec in scratch()],
        compiler_params=pltpu.CompilerParams(collective_id=0, has_side_effects=True, vmem_limit_bytes=VMEM_LIMIT),
    )(*args)
    vector = ((2, 1024), F32)
    outs = (
        ((1, 128, 1024), F32), ((1, 128, 1024), F32), vector, vector, vector, vector,
        ((2, 64, 384), F32), ((2, 256), F32), ((2, 128, 64), F32), vector,
        ((2, 64, 512), F32), ((2, 512), F32), ((2, 512, 64), F32), vector,
    )
    return pl.pallas_call(
        outputs_kernel,
        name="outputs",
        out_shape=[jax.ShapeDtypeStruct(shape, dtype) for shape, dtype in outs],
        in_specs=[vmem] * len(found),
        out_specs=[vmem] * len(outs),
        compiler_params=pltpu.CompilerParams(vmem_limit_bytes=VMEM_LIMIT),
    )(*found)


def solution(mesh):
    in_specs = (
        P("dp", "tensor", None),
        P("dp", None),
        P(),
        P(),
        P(),
        P(),
        P(None, "dp", "tensor"),
        P(None, "tensor"),
        P(None, "tensor", "dp"),
        P(),
        P(None, "dp", "tensor"),
        P(None, "tensor"),
        P(None, "tensor", "dp"),
        P(),
        P("dp", "tensor", None),
    )
    out_specs = (
        P("dp", "tensor", None),
        P("dp", "tensor", None),
        P(),
        P(),
        P(),
        P(),
        P(None, "dp", "tensor"),
        P(None, "tensor"),
        P(None, "tensor", "dp"),
        P(),
        P(None, "dp", "tensor"),
        P(None, "tensor"),
        P(None, "tensor", "dp"),
        P(),
    )
    return jax.shard_map(body, mesh=mesh, in_specs=in_specs, out_specs=out_specs, check_vma=False)
```

```python
import jax
import jax.numpy as jnp
from jax import lax
from jax.experimental import pallas as pl
from jax.experimental.pallas import tpu as pltpu
from jax.sharding import PartitionSpec as P

HD = 64
ROT = 16
LAYERS = 2
MESH = pl.DeviceIdType.MESH
BF = jnp.bfloat16
F32 = jnp.float32

epsilon = 1e-05
root_half = 0.7071067811865476
gauss_norm = 0.3989422804014327
masked_score = -1e30

QKV, EXP, MIX, ALL = 384, 896, 896, 1536
NT = (((1,), (1,)), ((), ()))
TN = (((0,), (0,)), ((), ()))
VMEM_LIMIT = 62 * 1024 * 1024
WINDOW = 640


def dot(a, b, dims=(((1,), (0,)), ((), ()))):
    return lax.dot_general(a, b, dims, preferred_element_type=F32)


def place(i, r, sign):
    outer, inner = lax.div(i, 4), lax.rem(i, 4)
    r_outer, r_inner = (r // 4, r % 4) if isinstance(r, int) else (lax.div(r, 4), lax.rem(r, 4))
    return lax.rem(outer + r_outer, 2) * 4 + lax.rem(inner + 4 + sign * r_inner, 4)


def rows_of(i, count):
    return pl.ds(pl.multiple_of(i * count, count), count)


def remote(src, dst, send_sem, recv_sem, device):
    return pltpu.make_async_remote_copy(
        src_ref=src,
        dst_ref=dst,
        send_sem=send_sem,
        recv_sem=recv_sem,
        device_id=device,
        device_id_type=MESH,
    )


def meet(devices):
    barrier = pltpu.get_barrier_semaphore()
    for device in devices:
        pl.semaphore_signal(barrier, inc=1, device_id=device, device_id_type=MESH)
    pl.semaphore_wait(barrier, len(devices))


def gelu_value(hidden):
    return 0.5 * hidden * (1.0 + lax.erf(hidden * root_half))


def gelu_both(hidden):
    half = 0.5 * (1.0 + lax.erf(hidden * root_half))
    return hidden * half, half + hidden * jnp.exp(-0.5 * hidden * hidden) * gauss_norm


def norm_parts(stream):
    centre = stream - jnp.mean(stream, axis=-1, keepdims=True)
    inv_std = lax.rsqrt(jnp.mean(centre * centre, axis=-1, keepdims=True) + epsilon)
    return centre * inv_std, inv_std


def mask_bias(seg_col, seg_row, ahead):
    shape = (seg_col.shape[0], seg_row.shape[1])
    key_place = lax.broadcasted_iota(jnp.int32, shape, 1)
    query_place = lax.broadcasted_iota(jnp.int32, shape, 0) + ahead
    keep = (seg_col == seg_row) & (key_place <= query_place)
    return jnp.where(keep, 0.0, masked_score)


def head_masks(rows):
    lane = lax.broadcasted_iota(jnp.int32, (rows, 2 * HD), 1)
    return lane < HD


def pick(first_head, value, head):
    zero = jnp.zeros_like(value)
    return jnp.where(first_head, value, zero) if head == 0 else jnp.where(first_head, zero, value)


def lookup(i, table):
    found = table[0]
    for k in range(1, len(table)):
        found = jnp.where(i == k, table[k], found)
    return found


class Gather:
    order = (0, 3, 1, 4, 2, 5, 7, 6)

    def __init__(self, dp, t, ref, send, recv):
        self.t, self.ref, self.s, self.r = t, ref, send, recv
        self.up, self.down, self.over = ((dp, place(t, r, 1)) for r in (1, 3, 4))

    def peers(self):
        return [self.up, self.down, self.over]

    def rows(self, r, half=None):
        first = place(self.t, r, 1) * 128
        if half is None:
            return pl.ds(pl.multiple_of(first, 128), 128)
        return pl.ds(pl.multiple_of(first + half * 64, 64), 64)

    def copy(self, k, r, half, device):
        part = self.ref.at[self.rows(r, half), :]
        return remote(part, part, self.s.at[k], self.r.at[k], device)

    def sends(self):
        return (
            (0, 0, None, self.up), (1, 0, None, self.down), (2, 0, None, self.over),
            (3, 3, 0, self.up), (4, 1, 1, self.down),
            (5, 4, None, self.up), (6, 4, None, self.down), (7, 2, None, self.over),
        )

    def send(self, k):
        self.copy(*self.sends()[k]).start()

    def came(self, k):
        r, half = ((3, None), (1, None), (4, None), (2, 0), (2, 1), (7, None), (5, None), (6, None))[k]
        self.copy(k, r, half, self.up).wait_recv()

    def begin(self):
        for k in range(3):
            self.send(k)

    def relay_one(self):
        self.came(0)
        self.send(3)
        self.came(1)
        self.send(4)
        self.came(2)
        self.send(5)
        self.send(6)

    def relay_two(self):
        self.came(3)
        self.came(4)
        self.send(7)

    def before(self, i):
        pl.when(i == 1)(self.relay_one)
        pl.when(i == 4)(self.relay_two)
        self.late(i)

    def late(self, i):
        @pl.when(i == 5)
        def _():
            self.came(5)
            self.came(6)

        pl.when(i == 7)(lambda: self.came(7))

    def end(self):
        for k in range(8):
            self.copy(*self.sends()[k]).wait_send()


class Scatter:
    order = (6, 5, 7, 2, 4, 1, 3, 0)

    def __init__(self, dp, t, part, got, total, send, recv):
        self.part, self.got, self.total, self.s, self.r = part, got, total, send, recv
        self.up, self.down, self.over = ((dp, place(t, r, 1)) for r in (1, 3, 4))

    def copy(self, k):
        slot, first, count, device = (
            (0, 0, 128, self.over), (1, 0, 128, self.up), (2, 0, 128, self.down),
            (3, 0, 64, self.up), (3, 64, 64, self.down),
            (4, 0, 128, self.over), (5, 0, 128, self.up), (6, 0, 128, self.down),
        )[k]
        return remote(
            self.part.at[slot * 128 + first : slot * 128 + first + count, :],
            self.got.at[k * 128 : k * 128 + count, :],
            self.s.at[k], self.r.at[k], device,
        )

    def add(self, k, first=0, count=128):
        self.copy(k).wait_recv()
        self.total[first : first + count, :] += self.got[k * 128 : k * 128 + count, :].astype(F32)

    def step(self, j, partial):
        self.total[...] = partial

        @pl.when(j == 3)
        def _():
            self.add(0)

        @pl.when(j == 4)
        def _():
            self.add(1)
            self.add(2)

        @pl.when(j == 5)
        def _():
            self.add(3, 0, 64)

        @pl.when(j == 6)
        def _():
            self.add(4, 64, 64)

        @pl.when(j < 7)
        def _():
            self.part[rows_of(j, 128), :] = self.total[...].astype(BF)

        for at, ks in ((0, (0,)), (1, (1,)), (2, (2,)), (3, (3, 4)), (4, (5,)), (5, (6,)), (6, (7,))):

            @pl.when(j == at)
            def _(ks=ks):
                for k in ks:
                    self.copy(k).start()

    def put(self, j, partial, hold, own):
        for k in range(3, 7):

            @pl.when(j == k)
            def _(k=k):
                for half in range(2):
                    at = (2 * (k - 3) + half) * 128
                    hold[at : at + 128, :] = partial[:, half * 512 : (half + 1) * 512]

        @pl.when(j == 7)
        def _():
            own[...] = partial

        @pl.when(j < 3)
        def _():
            self.part[rows_of(j, 128), :] = partial.astype(BF)

        for k in range(3):
            pl.when(j == k)(self.copy(k).start)

    def relay(self, j, hold, own):
        if j == 7:
            self.total[...] = own[...]
        else:
            for half in range(2):
                at = (2 * (j - 3) + half) * 128
                self.total[:, half * 512 : (half + 1) * 512] = hold[at : at + 128, :]
        for add in {3: ((0,),), 4: ((1,), (2,)), 5: ((3, 0, 64),), 6: ((4, 64, 64),)}.get(j, ()):
            self.add(*add)
        if j < 7:
            self.part[j * 128 : (j + 1) * 128, :] = self.total[...].astype(BF)
        for k in {3: (3, 4), 4: (5,), 5: (6,), 6: (7,)}.get(j, ()):
            self.copy(k).start()

    def sum(self):
        for k in (5, 6, 7):
            self.add(k)
        return self.total[...]

    def end(self):
        for k in range(8):
            self.copy(k).wait_send()


class WeightGather:
    def __init__(self, dp, t, src, target, columns, send, recv, hand_send, hand_recv):
        self.chip, self.core = lax.div(dp, 2), lax.rem(dp, 2)
        self.src, self.ref, self.columns = src.at[:, columns], target, columns
        self.s, self.r, self.hs, self.hr = send, recv, hand_send, hand_recv
        self.up, self.down, self.over = ((place(self.chip, r, 1) * 2 + self.core, t) for r in (1, 3, 4))
        self.sibling = (self.chip * 2 + 1 - self.core, t)

    def peers(self):
        return [self.up, self.down, self.over, self.sibling]

    def rows(self, r, half=None, other=False):
        core = 1 - self.core if other else self.core
        first = (place(self.chip, r, 1) * 2 + core) * 64
        if half is None:
            return pl.ds(pl.multiple_of(first, 64), 64)
        return pl.ds(pl.multiple_of(first + half * 32, 32), 32)

    def copy(self, k, r, half, device):
        part = self.ref.at[self.rows(r, half), self.columns]
        return remote(part if r else self.src, part, self.s.at[k], self.r.at[k], device)

    def sends(self):
        return (
            (0, 0, None, self.up), (1, 0, None, self.down), (2, 0, None, self.over),
            (3, 3, 0, self.up), (4, 1, 1, self.down),
            (5, 4, None, self.up), (6, 4, None, self.down),
            (7, 7, 0, self.up), (8, 5, 1, self.down),
        )

    def send(self, k):
        self.copy(*self.sends()[k]).start()

    def came(self, k):
        r, half = ((3, None), (1, None), (4, None), (2, 0), (2, 1), (7, None), (5, None), (6, 0), (6, 1))[k]
        self.copy(k, r, half, self.up).wait_recv()

    def hand(self, r):
        part = self.ref.at[self.rows(r), self.columns]
        return remote(part if r else self.src, part, self.hs.at[r], self.hr.at[r], self.sibling)

    def handed(self, r):
        part = self.ref.at[self.rows(r, None, True), self.columns]
        return remote(part, part, self.hs.at[r], self.hr.at[r], self.sibling)

    def begin(self):
        for k in range(3):
            self.send(k)
        self.hand(0).start()
        self.ref[self.rows(0), self.columns] = self.src[...]

    def relay_one(self):
        for k, r, onward in ((0, 3, (3,)), (1, 1, (4,)), (2, 4, (5, 6))):
            self.came(k)
            for m in onward:
                self.send(m)
            self.hand(r).start()

    def relay_two(self):
        self.came(3)
        self.came(4)
        self.hand(2).start()
        for k, r, onward in ((5, 7, 7), (6, 5, 8)):
            self.came(k)
            self.send(onward)
            self.hand(r).start()

    def relay_three(self):
        self.came(7)
        self.came(8)
        self.hand(6).start()

    def end(self):
        for r in range(8):
            self.handed(r).wait_recv()
            self.hand(r).wait_send()
        for k in range(9):
            self.copy(*self.sends()[k]).wait_send()


class GradSum:
    def __init__(self, dp, t, g_ref, out_ref, pair_ref, got_ref, p_send, p_recv, g_send, g_recv):
        self.chip, self.core = lax.div(dp, 2), lax.rem(dp, 2)
        self.up, self.down, self.over = ((place(self.chip, r, 1) * 2 + self.core, t) for r in (1, 3, 4))
        self.sibling = (self.chip * 2 + 1 - self.core, t)
        self.g, self.pair, self.got, self.out = g_ref, pair_ref, got_ref, out_ref
        self.p_send, self.p_recv, self.s, self.r = p_send, p_recv, g_send, g_recv

    def peers(self):
        return [self.up, self.down, self.over, self.sibling]

    def pair_copy(self):
        return remote(
            self.g.at[rows_of(1 - self.core, 512), :], self.pair, self.p_send.at[0], self.p_recv.at[0], self.sibling
        )

    def rows(self, r, half=None):
        first = place(self.chip, r, 1) * 64
        if half is None:
            return pl.ds(pl.multiple_of(first, 64), 64)
        return pl.ds(pl.multiple_of(first + half * 32, 32), 32)

    def copy(self, k):
        r, half, device = (
            (6, 0, self.up), (6, 1, self.down), (2, 0, self.up), (2, 1, self.down),
            (5, None, self.up), (7, None, self.down), (1, None, self.up), (3, None, self.down),
            (4, None, self.over),
        )[k]
        count = 64 if half is None else 32
        return remote(
            self.pair.at[self.rows(r, half), :],
            self.got.at[k * 64 : k * 64 + count, :],
            self.s.at[k], self.r.at[k], device,
        )

    def add(self, k, r, half=None):
        self.copy(k).wait_recv()
        count = 64 if half is None else 32
        rows = self.rows(r, half)
        arrived = self.got[k * 64 : k * 64 + count, :].astype(F32)
        self.pair[rows, :] = (self.pair[rows, :].astype(F32) + arrived).astype(BF)

    def begin(self):
        self.pair_copy().start()

    def one(self):
        self.pair_copy().wait()
        for r in (6, 2, 5, 7, 1, 3, 4, 0):
            rows = self.rows(r)
            own = self.g[rows_of(self.core * 8 + place(self.chip, r, 1), 64), :].astype(F32)
            both = self.pair[rows, :].astype(F32) + own
            if r:
                self.pair[rows, :] = both.astype(BF)
            else:
                self.out[...] = both
            for k in {6: (0, 1), 2: (2, 3)}.get(r, ()):
                self.copy(k).start()

    def two(self):
        for k, r, half in ((0, 5, 0), (1, 7, 1), (2, 1, 0), (3, 3, 1)):
            self.add(k, r, half)
            self.copy(k + 4).start()

    def three(self):
        self.add(4, 4)
        self.add(5, 4)
        self.copy(8).start()

    def end(self):
        for k in (6, 7, 8):
            self.copy(k).wait_recv()
            self.out[...] += self.got[k * 64 : (k + 1) * 64, :].astype(F32)
        for k in range(9):
            self.copy(k).wait_send()


class Bag:
    pass


def make_tables(seg_row_ref, m):
    seg = seg_row_ref[...].astype(F32)
    m.seg_row[...] = jnp.broadcast_to(seg, (8, 1024))
    first_place = jnp.zeros_like(seg)
    for value in range(3):
        count = jnp.sum((seg == value).astype(F32), axis=1, keepdims=True)
        first_place = first_place + jnp.where(seg > value, count, 0.0)
    offset = lax.broadcasted_iota(jnp.int32, (1, 1024), 1).astype(F32) - first_place
    which = lax.broadcasted_iota(jnp.int32, (8, 1), 0)
    frequency = lookup(which, [10000.0 ** (-2.0 * i / ROT) for i in range(ROT // 2)])
    angles = frequency * offset
    cosine, sine = jnp.cos(angles), jnp.sin(angles)
    lane = lax.broadcasted_iota(jnp.int32, (8, 128), 1)
    row = lax.broadcasted_iota(jnp.int32, (8, 128), 0)
    feature = lane & (HD - 1)
    same = (lane & 7) == row

    def spread(values, where, sign):
        choice = jnp.where(where, sign, 0.0)
        return lax.dot_general(values, choice, TN, preferred_element_type=F32, precision=lax.Precision.HIGHEST)

    still = ((lax.broadcasted_iota(jnp.int32, (1024, 128), 1) & (HD - 1)) >= ROT).astype(F32)
    m.cos[...] = spread(cosine, same & (feature < ROT), 1.0) + still
    m.sin1[...] = spread(sine, same & (feature < ROT // 2), -1.0)
    m.sin2[...] = spread(sine, same & (feature < ROT) & (feature >= ROT // 2), 1.0)
    m.columns[...] = spread(m.seg_row[...], row == 0, 1.0)


def window_of(c):
    return pl.multiple_of(lax.max(c - 4, 0) * 128, 128)


def window_bias(m, rows, c):
    start = window_of(c)
    return mask_bias(m.columns[rows, 0:1], m.seg_row[0:1, pl.ds(start, WINDOW)], c * 128 - start)


def rotate(x, m, rows):
    return (
        x * m.cos[rows, :]
        + pltpu.roll(x, 120, 1) * m.sin1[rows, :]
        + pltpu.roll(x, 8, 1) * m.sin2[rows, :]
    )


def unrotate(d, m, rows):
    return (
        d * m.cos[rows, :]
        - pltpu.roll(d, 120, 1) * m.sin1[rows, :]
        - pltpu.roll(d, 8, 1) * m.sin2[rows, :]
    )


def enter_forward(rows, vec, abias, ebias, m, L):
    hat = L.nhat[rows, :].astype(F32)
    one = (hat * vec[0:1, :] + vec[1:2, :]).astype(BF)
    two = (hat * vec[2:3, :] + vec[3:4, :]).astype(BF)
    projected = dot(one, L.w[:, :QKV]) + abias
    L.qkv[rows, 0:128] = (rotate(projected[:, 0:128], m, rows) * 0.125).astype(BF)
    L.qkv[rows, 128:256] = rotate(projected[:, 128:256], m, rows).astype(BF)
    L.qkv[rows, 256:384] = projected[:, 256:384].astype(BF)
    hidden = dot(two, L.w[:, QKV:EXP]) + ebias
    L.hidden[rows, :] = hidden
    L.ma[rows, 128:640] = gelu_value(hidden).astype(BF)


def attend_forward(c, rows, m, L):
    bias = window_bias(m, rows, c)
    keys_at = pl.ds(window_of(c), WINDOW)
    q = L.qkv[rows, 0:128]
    keys = L.qkv[keys_at, 128:256]
    values = L.qkv[keys_at, 256:384]
    first_head = head_masks(128)
    outs = []
    for head in range(2):
        scores = dot(pick(first_head, q, head), keys, NT) + bias
        row_max = jnp.max(scores, axis=-1, keepdims=True)
        exps = jnp.exp(scores - row_max)
        row_sum = jnp.sum(exps, axis=-1, keepdims=True)
        m.columns[rows, L.lse + head : L.lse + head + 1] = row_max + jnp.log(row_sum)
        outs.append(dot((exps * (1.0 / row_sum)).astype(BF), values))
    L.ma[rows, 0:128] = jnp.where(first_head, outs[0], outs[1]).astype(BF)


def enter_backward(rows, layer, m, L):
    back = dot(L.up_all[rows, :], L.w[:, MIX:ALL])
    m.mg[rows, :] = back[:, 0:128].astype(BF)
    _, slope = gelu_both(L.hidden[rows, :])
    hidden_grad = back[:, 128:640] * slope
    m.biases[layer : layer + 1, 256:768] += jnp.sum(hidden_grad, axis=0, keepdims=True)
    m.hh[rows, :] = hidden_grad.astype(BF)


def attend_backward(c, layer, m, L):
    rows = rows_of(c, 128)
    bias = window_bias(m, rows, c)
    keys_at = pl.ds(window_of(c), WINDOW)
    q = L.qkv[rows, 0:128]
    keys = L.qkv[keys_at, 128:256]
    values = L.qkv[keys_at, 256:384]
    out_grad = m.mg[rows, :]
    product = out_grad.astype(F32) * L.ma[rows, 0:128].astype(F32)
    first_head = head_masks(128)
    query_grads, key_grads, value_grads = [], [], []
    for head in range(2):
        scores = dot(pick(first_head, q, head), keys, NT) + bias
        soft = jnp.exp(scores - m.columns[rows, L.lse + head : L.lse + head + 1])
        prob_grad = dot(pick(first_head, out_grad, head), values, NT)
        delta = jnp.sum(pick(first_head, product, head), axis=-1, keepdims=True)
        score_grad = (soft * (prob_grad - delta)).astype(BF)
        query_grads.append(dot(score_grad, keys))
        key_grads.append(dot(score_grad, q, TN))
        value_grads.append(dot(soft.astype(BF), out_grad, TN))
    wide_first = head_masks(WINDOW)
    m.dk[keys_at, :] += jnp.where(wide_first, key_grads[0], key_grads[1])
    m.dv[keys_at, :] += jnp.where(wide_first, value_grads[0], value_grads[1])
    query_grad = unrotate(jnp.where(first_head, query_grads[0], query_grads[1]) * 0.125, m, rows)
    m.biases[layer : layer + 1, 0:128] += jnp.sum(query_grad, axis=0, keepdims=True)
    m.pg[rows, 0:128] = query_grad.astype(BF)


def close_attention(c, layer, m):
    rows = rows_of(c, 128)
    m.pg[rows, 128:256] = unrotate(m.dk[rows, :], m, rows).astype(BF)
    value_grad = m.dv[rows, :]
    m.biases[layer : layer + 1, 128:256] += jnp.sum(value_grad, axis=0, keepdims=True)
    m.pg[rows, 256:384] = value_grad.astype(BF)


def leave_backward(rows, layer, vec, m, L):
    first_grad = dot(m.pg[rows, :], L.w[:, :QKV], NT)
    second_grad = dot(m.hh[rows, :], L.w[:, QKV:EXP], NT)
    hat = L.nhat[rows, :].astype(F32)
    for k, value in enumerate((first_grad * hat, first_grad, second_grad * hat, second_grad)):
        at = 5 * layer + k
        m.small[at : at + 1, :] += jnp.sum(value, axis=0, keepdims=True)
    return first_grad * vec[0:1, :] + second_grad * vec[2:3, :]


def put_by_owner(target, i, value, columns):
    target[rows_of(i, 64), columns] = value[0:64].astype(BF)
    target[rows_of(i + 8, 64), columns] = value[64:128].astype(BF)


def weight_grads(kind, vec, m, L):
    def step(i, carry):
        at = pl.ds(pl.multiple_of(i * 128, 128), 128)
        if kind == "out":
            put_by_owner(L.g_ff, i, dot(L.up_all[:, at], L.ma[...], TN), slice(512, 1152))
        else:
            k = 0 if kind == "in" else 2
            normed = (L.nhat[:, at].astype(F32) * vec[k : k + 1, at] + vec[k + 1 : k + 2, at]).astype(BF)
            if kind == "in":
                put_by_owner(L.g_in, i, dot(normed, m.pg[...], TN), slice(0, 384))
            else:
                put_by_owner(L.g_ff, i, dot(normed, m.hh[...], TN), slice(0, 512))
        return carry

    lax.fori_loop(0, 8, step, 0)


class Sums:
    def __init__(self, dp, t, m):
        self.dp, self.t, self.m = dp, t, m

    def tensor_peer(self, r):
        return (self.dp, place(self.t, r, 1))

    def dp_peer(self, r):
        return (lax.rem(self.dp + r, 16), self.t)

    def peers(self):
        return [self.tensor_peer(r) for r in range(1, 8)] + [self.dp_peer(r) for r in range(1, 16)]

    def lanes(self, i):
        return pl.ds(pl.multiple_of(i * 128, 128), 128)

    def bias_copy(self, r, came=False):
        m = self.m
        at = rows_of(lax.rem(self.dp + 16 - r, 16), 8) if came else rows_of(self.dp, 8)
        src = m.all_biases.at[at, :] if came else m.biases
        return remote(src, m.all_biases.at[at, :], m.e_send.at[r], m.e_recv.at[r], self.dp_peer(r))

    def t_copy(self, r, came=False):
        m, to = self.m, place(self.t, r, 1)
        at = rows_of(place(self.t, r, -1), 16) if came else rows_of(self.t, 16)
        return remote(m.small.at[:, self.lanes(to)], m.t_all.at[at, :], m.t_send.at[r], m.t_recv.at[r], self.tensor_peer(r))

    def d_copy(self, r, came=False):
        m = self.m
        at = rows_of(lax.rem(self.dp + 16 - r, 16), 16) if came else rows_of(self.dp, 16)
        return remote(m.d_all.at[at, :], m.d_all.at[at, :], m.d_send.at[r], m.d_recv.at[r], self.dp_peer(r))

    def u_copy(self, r, came=False):
        m = self.m
        at = self.lanes(place(self.t, r, -1) if came else self.t)
        return remote(m.total.at[:, at], m.total.at[:, at], m.u_send.at[r], m.u_recv.at[r], self.tensor_peer(r))

    def send_biases(self):
        self.m.all_biases[rows_of(self.dp, 8), :] = self.m.biases[...]
        for r in range(1, 16):
            self.bias_copy(r).start()

    def begin(self):
        self.m.t_all[rows_of(self.t, 16), :] = self.m.small[:, self.lanes(self.t)]
        for r in range(1, 8):
            self.t_copy(r).start()

    def over_dp(self):
        m = self.m
        for r in range(1, 8):
            self.t_copy(r, True).wait_recv()
        total = m.t_all[0:16, :]
        for i in range(1, 8):
            total = total + m.t_all[i * 16 : (i + 1) * 16, :]
        m.d_all[rows_of(self.dp, 16), :] = total
        for r in range(1, 16):
            self.d_copy(r).start()

    def back(self):
        m = self.m
        for r in range(1, 16):
            self.d_copy(r, True).wait_recv()
        total = m.d_all[0:16, :]
        for i in range(1, 16):
            total = total + m.d_all[i * 16 : (i + 1) * 16, :]
        m.total[:, self.lanes(self.t)] = total
        for r in range(1, 8):
            self.u_copy(r).start()

    def end(self):
        m = self.m
        for r in range(1, 16):
            self.bias_copy(r, True).wait_recv()
        total = m.all_biases[0:8, :]
        for i in range(1, 16):
            total = total + m.all_biases[i * 8 : (i + 1) * 8, :]
        m.bias_total[...] = total
        for r in range(1, 8):
            self.u_copy(r, True).wait_recv()
        for r in range(1, 8):
            self.t_copy(r).wait_send()
            self.u_copy(r).wait_send()
        for r in range(1, 16):
            self.d_copy(r).wait_send()
            self.bias_copy(r).wait_send()


INPUTS = (
    ("residual", (128, 1024), BF),
    ("seg_in", (1, 1024), jnp.int32),
    ("gain1", (2, 1024), F32),
    ("bias1", (2, 1024), F32),
    ("gain2", (2, 1024), F32),
    ("bias2", (2, 1024), F32),
    ("attention_weight", (2, 64, 384), BF),
    ("attention_bias", (2, 256), F32),
    ("project_weight", (2, 64, 128), BF),
    ("project_bias", (2, 1024), F32),
    ("expand_weight", (2, 64, 512), BF),
    ("ebias", (2, 512), F32),
    ("contract_weight", (2, 64, 512), BF),
    ("contract_bias", (2, 1024), F32),
    ("cotangent", (128, 1024), F32),
)
OUTPUTS = (
    ("result", (128, 1024), F32),
    ("residual_grad", (128, 1024), F32),
    ("ff_sum0", (64, 1152), F32),
    ("in_sum0", (64, 384), F32),
    ("ff_sum1", (64, 1152), F32),
    ("in_sum1", (64, 384), F32),
    ("total", (16, 1024), F32),
    ("bias_total", (8, 768), F32),
)


def dma(*shape):
    return pltpu.SemaphoreType.DMA(shape)


def scratch():
    vmem = pltpu.VMEM
    found = [(name, vmem(shape, dtype)) for name, shape, dtype in INPUTS] + [
        ("in_sems", dma(len(INPUTS))),
        ("packed", vmem((2, 64, ALL), BF)),
        ("vec", vmem((2, 8, 1024), F32)),
        ("abias", vmem((2, 384), F32)),
        ("seg_row", vmem((8, 1024), F32)),
        ("cos", vmem((1024, 128), F32)),
        ("sin1", vmem((1024, 128), F32)),
        ("sin2", vmem((1024, 128), F32)),
        ("columns", vmem((1024, 128), F32)),
        ("stream", vmem((128, 1024), F32)),
        ("up", vmem((128, 1024), F32)),
        ("part", vmem((1024, 1024), BF)),
        ("sum", vmem((128, 1024), F32)),
        ("mg", vmem((1024, 128), BF)),
        ("hh", vmem((1024, 512), BF)),
        ("pg", vmem((1024, 384), BF)),
        ("dk", vmem((1024, 128), F32)),
        ("dv", vmem((1024, 128), F32)),
        ("small", vmem((16, 1024), F32)),
        ("biases", vmem((8, 768), F32)),
        ("all_biases", vmem((128, 768), F32)),
        ("t_all", vmem((128, 128), F32)),
        ("d_all", vmem((256, 128), F32)),
        ("e_send", dma(16)), ("e_recv", dma(16)),
        ("t_send", dma(8)), ("t_recv", dma(8)),
        ("d_send", dma(16)), ("d_recv", dma(16)),
        ("u_send", dma(8)), ("u_recv", dma(8)),
        ("ag_send", dma(4, 8)), ("ag_recv", dma(4, 8)),
        ("rs_send", dma(4, 8)), ("rs_recv", dma(4, 8)),
        ("w_send", dma(3, 9)), ("w_recv", dma(3, 9)),
        ("wh_send", dma(3, 8)), ("wh_recv", dma(3, 8)),
        ("p_send", dma(4, 1)), ("p_recv", dma(4, 1)),
        ("g_send", dma(4, 9)), ("g_recv", dma(4, 9)),
    ]
    for layer in range(LAYERS):
        found += [
            (f"{name}{layer}", vmem(shape, dtype))
            for name, shape, dtype in (
                ("w", (1024, ALL), BF),
                ("nhat", (1024, 1024), BF),
                ("up_all", (1024, 1024), BF),
                ("qkv", (1024, 384), BF),
                ("ma", (1024, 640), BF),
                ("hidden", (1024, 512), F32),
                ("got_f", (1024, 1024), BF),
                ("got_b", (1024, 1024), BF),
                ("g_ff", (1024, 1152), BF),
                ("g_in", (1024, 384), BF),
                ("pair_ff", (512, 1152), BF),
                ("pair_in", (512, 384), BF),
                ("got_ff", (576, 1152), BF),
                ("got_in", (576, 384), BF),
            )
        ]
    return found


def by_part(columns):
    return jnp.concatenate([columns[:, k * HD : (k + 1) * HD] for k in (0, 3, 1, 4, 2, 5)], axis=1)


def by_head(columns):
    return jnp.concatenate([columns[:, k * HD : (k + 1) * HD] for k in (0, 2, 4, 1, 3, 5)], axis=1)


def pack(m):
    for layer in range(LAYERS):
        m.packed[layer, :, 0:384] = by_part(m.attention_weight[layer])
        m.packed[layer, :, 384:896] = m.expand_weight[layer]
        m.packed[layer, :, 896:1024] = m.project_weight[layer]
        m.packed[layer, :, 1024:1536] = m.contract_weight[layer]


def whole_kernel(*refs):
    m = Bag()
    taken = [name for name, _, _ in INPUTS]
    names = [f"far_{name}" for name in taken] + [o[0] for o in OUTPUTS] + [k for k, _ in scratch()]
    for name, ref in zip(names, refs, strict=True):
        setattr(m, name, ref)

    def fetch(name):
        far = getattr(m, f"far_{name}")
        near = getattr(m, name)
        far = far if far.shape == near.shape else far.at[0]
        return pltpu.make_async_copy(far, near, m.in_sems.at[taken.index(name)])

    early = ["attention_weight", "project_weight", "expand_weight", "contract_weight", "residual"]
    later = [name for name in taken if name not in early]
    for name in early + later:
        fetch(name).start()
    layers = []
    for layer in range(LAYERS):
        L = Bag()
        for name in ("w", "nhat", "up_all", "qkv", "ma", "hidden", "g_ff", "g_in"):
            setattr(L, name, getattr(m, f"{name}{layer}"))
        L.lse = 4 + 2 * layer
        L.vec = m.vec.at[layer]
        L.abias = m.abias.at[layer : layer + 1, :]
        L.ebias = m.ebias.at[layer : layer + 1, :]
        layers.append(L)
    first, second = layers
    dp, t = lax.axis_index("dp"), lax.axis_index("tensor")

    def gather(k, ref):
        return Gather(dp, t, ref, m.ag_send.at[k], m.ag_recv.at[k])

    def scatter(k, got):
        return Scatter(dp, t, m.part, got, m.sum, m.rs_send.at[k], m.rs_recv.at[k])

    def grad_sum(k, g, out, pair, got):
        return GradSum(dp, t, g, out, pair, got, m.p_send.at[k], m.p_recv.at[k], m.g_send.at[k], m.g_recv.at[k])

    parts = ((0, slice(0, EXP)), (0, slice(EXP, ALL)), (1, slice(0, ALL)))
    weights = [
        WeightGather(
            dp, t, m.packed.at[layer], layers[layer].w, columns,
            m.w_send.at[k], m.w_recv.at[k], m.wh_send.at[k], m.wh_recv.at[k],
        )
        for k, (layer, columns) in enumerate(parts)
    ]
    hats = [gather(k, layers[k].nhat) for k in range(2)]
    ups = [gather(2 + k, layers[k].up_all) for k in range(2)]
    outs = [scatter(0, m.got_f0), scatter(1, m.got_f1)]
    backs = [scatter(2, m.got_b0), scatter(3, m.got_b1)]
    ff = [
        grad_sum(0, m.g_ff0, m.ff_sum0, m.pair_ff0, m.got_ff0),
        grad_sum(1, m.g_ff1, m.ff_sum1, m.pair_ff1, m.got_ff1),
    ]
    inn = [
        grad_sum(2, m.g_in0, m.in_sum0, m.pair_in0, m.got_in0),
        grad_sum(3, m.g_in1, m.in_sum1, m.pair_in1, m.got_in1),
    ]
    sums = Sums(dp, t, m)
    for name in early:
        fetch(name).wait()
    pack(m)
    meet(sums.peers())

    def at_block(table, j):
        c = place(t, lookup(j, table), 1)
        return c, rows_of(c, 128)

    weights[0].begin()
    stream0 = m.residual[...].astype(F32)
    mine = rows_of(t, 128)
    first.nhat[mine, :] = norm_parts(stream0)[0].astype(BF)
    hats[0].begin()
    for name in later:
        fetch(name).wait()
    second.up_all[mine, :] = m.cotangent[...].astype(BF)
    m.small[...] = jnp.zeros_like(m.small)
    m.biases[...] = jnp.zeros_like(m.biases)
    m.vec[...] = jnp.zeros_like(m.vec)
    for k, value in enumerate((m.gain1, m.bias1, m.gain2, m.bias2)):
        for layer in range(LAYERS):
            m.vec[layer, k : k + 1, :] = value[layer : layer + 1, :]
    for layer in range(LAYERS):
        m.vec[layer, 4:5, :] = m.project_bias[layer : layer + 1, :] + m.contract_bias[layer : layer + 1, :]
    pairs = m.attention_bias[...]
    m.abias[:, 0:128] = jnp.concatenate([pairs[:, 0:64], pairs[:, 128:192]], axis=1)
    m.abias[:, 128:256] = jnp.zeros((2, 128), F32)
    m.abias[:, 256:384] = jnp.concatenate([pairs[:, 64:128], pairs[:, 192:256]], axis=1)
    make_tables(m.seg_in, m)
    weights[0].relay_one()
    hats[0].relay_one()
    weights[1].begin()
    weights[0].relay_two()
    hats[0].relay_two()
    ups[1].begin()
    weights[0].relay_three()
    weights[0].end()
    weights[1].relay_one()

    def enter0(i, carry):
        hats[0].late(i)
        enter_forward(at_block(Gather.order, i)[1], first.vec, first.abias[...], first.ebias[...], m, first)
        pl.when(i == 4)(weights[1].relay_two)
        return carry

    lax.fori_loop(0, 8, enter0, 0)
    ups[1].relay_one()
    weights[1].relay_three()
    weights[1].end()
    weights[2].begin()

    def attend0(j, carry):
        c, rows = at_block(Scatter.order, j)
        attend_forward(c, rows, m, first)
        outs[0].step(j, dot(first.ma[rows, :], first.w[:, MIX:ALL], NT))
        pl.when(j == 3)(weights[2].relay_one)
        pl.when(j == 4)(ups[1].relay_two)
        pl.when(j == 6)(weights[2].relay_two)
        return carry

    lax.fori_loop(0, 8, attend0, 0)
    stream1 = outs[0].sum() + m.residual[...].astype(F32) + first.vec[4:5, :]
    m.stream[...] = stream1

    second.nhat[mine, :] = norm_parts(stream1)[0].astype(BF)
    hats[1].begin()
    weights[2].relay_three()
    outs[0].end()
    weights[2].end()

    def enter1(i, carry):
        hats[1].before(i)
        enter_forward(at_block(Gather.order, i)[1], second.vec, second.abias[...], second.ebias[...], m, second)
        return carry

    lax.fori_loop(0, 8, enter1, 0)

    def attend1(j, carry):
        c, rows = at_block(Scatter.order, j)
        attend_forward(c, rows, m, second)
        outs[1].step(j, dot(second.ma[rows, :], second.w[:, MIX:ALL], NT))
        return carry

    lax.fori_loop(0, 8, attend1, 0)

    def back_through(layer, L, start, early, middle, late):
        own = m.up if layer else m.cotangent
        m.dk[...] = jnp.zeros_like(m.dk)
        m.dv[...] = jnp.zeros_like(m.dv)

        def enter(i, carry):
            if layer == 0:
                ups[0].late(i)
            enter_backward(at_block(Gather.order, i)[1], layer, m, L)
            return carry

        lax.fori_loop(0, 8, enter, 0)
        start()

        def attend(c, carry):
            attend_backward(c, layer, m, L)
            early(c)
            return carry

        lax.fori_loop(0, 8, attend, 0)

        def close(c, carry):
            close_attention(c, layer, m)
            return carry

        lax.fori_loop(0, 8, close, 0)
        middle()

        def leave(j, carry):
            rows = at_block(Scatter.order, j)[1]
            backs[layer].put(j, leave_backward(rows, layer, L.vec, m, L), m.hidden1, own)
            return carry

        lax.fori_loop(0, 8, leave, 0)
        for j in range(3, 8):
            backs[layer].relay(j, m.hidden1, own)
            late(j)

    def to_stream(layer, up, stream):
        hat_grad = backs[layer].sum()
        hat, inv_std = norm_parts(stream)
        return up + inv_std * (
            hat_grad
            - jnp.mean(hat_grad, axis=-1, keepdims=True)
            - hat * jnp.mean(hat_grad * hat, axis=-1, keepdims=True)
        )

    def nothing(*_):
        pass

    ups[1].came(5)
    ups[1].came(6)
    ups[1].came(7)
    m.small[9:10, :] = jnp.sum(m.cotangent[...], axis=0, keepdims=True)

    def result():
        m.result[...] = outs[1].sum() + m.stream[...] + second.vec[4:5, :]
        outs[1].end()

    def late1(j):
        if j == 3:
            weight_grads("out", second.vec, m, second)

    back_through(1, second, result, nothing, nothing, late1)
    up = to_stream(1, m.cotangent[...], m.stream[...])
    m.up[...] = up
    first.up_all[mine, :] = up.astype(BF)
    ups[0].begin()
    m.small[4:5, :] = jnp.sum(up, axis=0, keepdims=True)
    weight_grads("expand", second.vec, m, second)
    ff[1].begin()
    backs[1].end()
    ups[0].relay_one()
    weight_grads("in", second.vec, m, second)
    inn[1].begin()
    ff[1].one()
    ups[0].relay_two()
    inn[1].one()

    def start0():
        ff[1].two()
        inn[1].two()
        weight_grads("out", first.vec, m, first)
        weight_grads("expand", first.vec, m, first)
        ff[0].begin()

    def early0(c):
        @pl.when(c == 2)
        def _():
            ff[1].three()
            inn[1].three()
            ff[0].one()

        pl.when(c == 6)(ff[0].two)

    def late0(j):
        if j == 3:
            sums.begin()
            weight_grads("in", first.vec, m, first)
            inn[0].begin()
        if j == 5:
            sums.over_dp()
        if j == 6:
            ff[0].three()
            inn[0].one()

    back_through(0, first, start0, early0, sums.send_biases, late0)
    sums.back()
    ff[1].end()
    inn[1].end()
    inn[0].two()
    m.residual_grad[...] = to_stream(0, m.up[...], m.residual[...].astype(F32))
    inn[0].three()
    ff[0].end()
    inn[0].end()
    sums.end()
    backs[0].end()
    for each in hats + ups:
        each.end()


def outputs_kernel(
    result, residual_grad, ff0, in0, ff1, in1, total, bias_total,
    result_out, residual_grad_out, gain1, bias1, gain2, bias2,
    attention_weight, attention_bias, project_weight, project_bias, expand_weight, expand_bias, contract_weight, contract_bias,
):
    result_out[0] = result[...]
    residual_grad_out[0] = residual_grad[...]
    for layer, (ff, inn) in enumerate(((ff0, in0), (ff1, in1))):
        for k, out in enumerate((gain1, bias1, gain2, bias2, project_bias)):
            out[layer : layer + 1, :] = total[5 * layer + k : 5 * layer + k + 1, :]
        contract_bias[layer : layer + 1, :] = total[5 * layer + 4 : 5 * layer + 5, :]
        attention_weight[layer] = by_head(inn[...])
        expand_weight[layer] = ff[:, 0:512]
        project_weight[layer] = ff[:, 512:640]
        contract_weight[layer] = ff[:, 640:1152]
    biases = bias_total[0:2, :]
    attention_bias[...] = jnp.concatenate(
        [biases[:, k * HD : (k + 1) * HD] for k in (0, 2, 1, 3)], axis=1
    )
    expand_bias[...] = biases[:, 256:768]


def body(
    residual,
    segments,
    first_gain,
    first_bias,
    second_gain,
    second_bias,
    attention_weight,
    attention_bias,
    project_weight,
    project_bias,
    expand_weight,
    expand_bias,
    contract_weight,
    contract_bias,
    cotangent,
):
    args = (
        residual,
        segments,
        first_gain,
        first_bias,
        second_gain,
        second_bias,
        attention_weight,
        attention_bias,
        project_weight.swapaxes(1, 2),
        project_bias,
        expand_weight,
        expand_bias,
        contract_weight.swapaxes(1, 2),
        contract_bias,
        cotangent,
    )
    vmem = pl.BlockSpec(memory_space=pltpu.VMEM)
    found = pl.pallas_call(
        whole_kernel,
        name="layers",
        out_shape=[jax.ShapeDtypeStruct(shape, dtype) for _, shape, dtype in OUTPUTS],
        in_specs=[pl.BlockSpec(memory_space=pl.ANY)] * len(args),
        out_specs=[vmem] * len(OUTPUTS),
        scratch_shapes=[spec for _, spec in scratch()],
        compiler_params=pltpu.CompilerParams(collective_id=0, has_side_effects=True, vmem_limit_bytes=VMEM_LIMIT),
    )(*args)
    vector = ((2, 1024), F32)
    outs = (
        ((1, 128, 1024), F32), ((1, 128, 1024), F32), vector, vector, vector, vector,
        ((2, 64, 384), F32), ((2, 256), F32), ((2, 64, 128), F32), vector,
        ((2, 64, 512), F32), ((2, 512), F32), ((2, 64, 512), F32), vector,
    )
    made = pl.pallas_call(
        outputs_kernel,
        name="outputs",
        out_shape=[jax.ShapeDtypeStruct(shape, dtype) for shape, dtype in outs],
        in_specs=[vmem] * len(found),
        out_specs=[vmem] * len(outs),
        compiler_params=pltpu.CompilerParams(vmem_limit_bytes=VMEM_LIMIT),
    )(*found)
    return tuple(value.swapaxes(1, 2) if k in (8, 12) else value for k, value in enumerate(made))


def solution(mesh):
    in_specs = (
        P("dp", "tensor", None),
        P("dp", None),
        P(),
        P(),
        P(),
        P(),
        P(None, "dp", "tensor"),
        P(None, "tensor"),
        P(None, "tensor", "dp"),
        P(),
        P(None, "dp", "tensor"),
        P(None, "tensor"),
        P(None, "tensor", "dp"),
        P(),
        P("dp", "tensor", None),
    )
    out_specs = (
        P("dp", "tensor", None),
        P("dp", "tensor", None),
        P(),
        P(),
        P(),
        P(),
        P(None, "dp", "tensor"),
        P(None, "tensor"),
        P(None, "tensor", "dp"),
        P(),
        P(None, "dp", "tensor"),
        P(None, "tensor"),
        P(None, "tensor", "dp"),
        P(),
    )
    return jax.shard_map(body, mesh=mesh, in_specs=in_specs, out_specs=out_specs, check_vma=False)
```
